32 devices in a mesh: seq: 2 (over x), ffn: 16 (over z, y, core).
Axes of the slice: x: 2, y: 2, z: 4, core: 2. Of those that a mesh axis runs over, the one named last changes fastest.
Arguments:
- hidden_in: bfloat16 [20480, 768], P(('seq', 'ffn')), may hold values from -6 to 6
- doc_lengths: int32 [2, 32], P('seq'), may hold values from 79 to 561, as said below
- box_x: int32 [20480], P('seq'), may hold values from 0 to 1000
- box_y: int32 [20480], P('seq'), may hold values from 0 to 1000
- token_valid: int32 [20480], P('seq'), may hold values from 0 to 1, as said below
- w_query: bfloat16 [768, 768], replicated, may hold values from -0.21875 to 0.21875
- b_query: bfloat16 [768], replicated, may hold values from -1.75 to 1.75
- w_key: bfloat16 [768, 768], replicated, may hold values from -0.21875 to 0.21875
- w_value: bfloat16 [768, 768], replicated, may hold values from -0.21875 to 0.21875
- b_value: bfloat16 [768], replicated, may hold values from -1.75 to 1.75
- w_out: bfloat16 [768, 768], replicated, may hold values from -3 to 3
- b_out: bfloat16 [768], replicated, may hold values from -1.75 to 1.75
- gain_attn: bfloat16 [768], replicated, may hold values from 0.5 to 1.5
- shift_attn: bfloat16 [768], replicated, may hold values from -1.75 to 1.75
- w_up: bfloat16 [768, 3072], P(None, 'ffn'), may hold values from -0.21875 to 0.21875
- b_up: bfloat16 [3072], P('ffn'), may hold values from -1.75 to 1.75
- w_down: bfloat16 [3072, 768], P('ffn'), may hold values from -0.109375 to 0.109375
- b_down: bfloat16 [768], replicated, may hold values from -1.75 to 1.75
- gain_out: bfloat16 [768], replicated, may hold values from 0.5 to 1.5
- shift_out: bfloat16 [768], replicated, may hold values from -1.75 to 1.75
- table_seq: bfloat16 [32, 12], replicated, may hold values from -6 to 6
- table_x: bfloat16 [64, 12], replicated, may hold values from -6 to 6
- table_y: bfloat16 [64, 12], replicated, may hold values from -6 to 6
- out_grad: bfloat16 [20480, 768], P(('seq', 'ffn')), may hold values from -6 to 6
Outputs:
- hidden_out: float32 [20480, 768], P(('seq', 'ffn'))
- hidden_grad: float32 [20480, 768], P(('seq', 'ffn'))
- grad_w_query: float32 [768, 768], replicated
- grad_b_query: float32 [768], replicated
- grad_w_key: float32 [768, 768], replicated
- grad_w_value: float32 [768, 768], replicated
- grad_b_value: float32 [768], replicated
- grad_w_out: float32 [768, 768], replicated
- grad_b_out: float32 [768], replicated
- grad_gain_attn: float32 [768], replicated
- grad_shift_attn: float32 [768], replicated
- grad_w_up: float32 [768, 3072], P(None, 'ffn')
- grad_b_up: float32 [3072], P('ffn')
- grad_w_down: float32 [3072, 768], P('ffn')
- grad_b_down: float32 [768], replicated
- grad_gain_out: float32 [768], replicated
- grad_shift_out: float32 [768], replicated
- grad_table_seq: float32 [32, 12], replicated
- grad_table_x: float32 [64, 12], replicated
- grad_table_y: float32 [64, 12], replicated
The draws below stay inside these ranges and needn't reach their ends.
Inputs may be any that keep to these rules, and one draw needn't show every extreme that they name: `doc_lengths`: each row holds the lengths of the 32 documents of one pack, in order; they sum to 10240. Every pack has a document of the most and one of the least length. `token_valid`: padding rows are the last rows of their document, at most half of those after its first 49 rows, which are never padding.
All inputs are finite; a program needn't handle non-finite values.
Results may differ from the reference program's by a relative error of at most 0.014.
Values may be sent and summed in bfloat16 or wider, within the bound.
A program may use at most 448 MiB of HBM per device.

```python
import jax
import jax.numpy as jnp
from jax import lax

D = 768
HEADS = 12
HEAD_DIM = 64
FF = 3072
BUCKETS_SEQ = 32
BUCKETS_BOX = 64
MAX_TEXT = 512
VISUAL = 49
MEAN_LEN = 320
KEY_BLOCK = 640
TOK_DEV = 640
DOCS = 32
TOKENS = 20480
N_SEQ = 2
N_FFN = 16


def packing(key):

    def one_group(group_key):
        first, second, third, fourth = jax.random.split(group_key, 4)
        group_rows = TOK_DEV * N_FFN
        longest = VISUAL + MAX_TEXT
        shortest = 2 * MEAN_LEN - longest
        half = DOCS // 2
        draws = jnp.minimum(jax.random.randint(first, (half,), shortest, longest + 1), jax.random.randint(fourth, (half,), shortest, longest + 1))
        draws = jnp.where(jnp.arange(half) == 0, longest, draws)
        paired = jnp.concatenate([draws, 2 * MEAN_LEN - draws])
        order = jax.random.permutation(second, DOCS)
        lengths = paired[order].astype(jnp.int32)
        padding = jax.random.randint(third, (DOCS,), 0, (lengths - VISUAL) // 2 + 1)
        ends = jnp.cumsum(lengths)
        row_ids = jnp.arange(group_rows, dtype=jnp.int32)
        doc_index = jnp.sum((row_ids[:, None] >= ends[None, :]).astype(jnp.int32), axis=1)
        starts = ends - lengths
        offset = row_ids - starts[doc_index]
        valid = (offset < (lengths - padding)[doc_index]).astype(jnp.int32)
        return (lengths, valid)
    return jax.vmap(one_group)(jax.random.split(key, N_SEQ))


def draw_doc_lengths(key, part):
    shared = packing(key)
    return shared[0].astype(jnp.int32)


def draw_token_valid(key, part):
    shared = packing(key)
    return shared[1].reshape(-1).astype(jnp.int32)


def set_ends(values, stream_key, smallest, high):
    dims = values.shape
    index_at = [jax.random.randint(jax.random.fold_in(stream_key, axis), (), 0, dims[axis]) for axis in range(len(dims))]
    values = values.at[tuple(index_at)].set(smallest)
    longest = dims.index(max(dims))
    index_at[longest] = (index_at[longest] + 1) % dims[longest]
    return values.at[tuple(index_at)].set(high)


def shard_levels(own_key, shape, shards, smallest, top_value):
    level, own = 1.0, jax.random.fold_in(own_key, 6)
    for position, shards_of in shards:
        steps = jnp.exp(jax.random.uniform(jax.random.fold_in(own, position), (shards_of,), jnp.float32, smallest / len(shards), top_value / len(shards)))
        level = level * jnp.repeat(steps, shape[position] // shards_of).reshape([-1 if axis == position else 1 for axis in range(len(shape))])
    return level


def normal_values(stream_key, extent, width, most, cuts=(), kind=jnp.bfloat16):
    drawn = jax.random.normal(stream_key, extent, jnp.float32) * width
    if len(cuts) > 0:
        drawn = shard_levels(stream_key, extent, cuts, -0.22, 0.18) * drawn
    return jnp.clip(drawn, min=-most, max=most).astype(kind)


def setup_inputs(seed: int = 0) -> dict:
    splits = jax.random.split(jax.random.key(seed), 25)
    hidden_in = normal_values(splits[0], (TOKENS, D), 1.0, 6.0, ((0, 32),))
    doc_lengths = draw_doc_lengths(jax.random.fold_in(splits[24], 71), 0)
    box_x = set_ends(jax.random.randint(splits[2], (TOKENS,), 0, 1001), jax.random.fold_in(splits[2], 1), 0, 1000).astype(jnp.int32)
    box_y = set_ends(jax.random.randint(splits[3], (TOKENS,), 0, 1001), jax.random.fold_in(splits[3], 1), 0, 1000).astype(jnp.int32)
    token_valid = draw_token_valid(jax.random.fold_in(splits[24], 71), 0)
    w_query = normal_values(splits[5], (D, D), D ** -0.5, 0.21875)
    b_query = normal_values(splits[6], (D,), 0.3, 1.75)
    w_key = normal_values(splits[7], (D, D), D ** -0.5, 0.21875)
    w_value = normal_values(splits[8], (D, D), D ** -0.5, 0.21875)
    b_value = normal_values(splits[9], (D,), 0.3, 1.75)
    w_out = normal_values(splits[10], (D, D), (max(D // 192, 1)) ** -0.5, 3.0)
    b_out = normal_values(splits[11], (D,), 0.3, 1.75)
    gain_attn = jnp.clip(1.0 + 0.1 * jax.random.normal(splits[12], (D,), jnp.float32), 0.5, 1.5).astype(jnp.bfloat16)
    shift_attn = normal_values(splits[13], (D,), 0.3, 1.75)
    w_up = normal_values(splits[14], (D, FF), D ** -0.5, 0.21875, ((1, 16),))
    b_up = normal_values(splits[15], (FF,), 0.3, 1.75, ((0, 16),))
    w_down = normal_values(splits[16], (FF, D), FF ** -0.5, 0.109375, ((0, 16),))
    b_down = normal_values(splits[17], (D,), 0.3, 1.75)
    gain_out = jnp.clip(1.0 + 0.1 * jax.random.normal(splits[18], (D,), jnp.float32), 0.5, 1.5).astype(jnp.bfloat16)
    shift_out = normal_values(splits[19], (D,), 0.3, 1.75)
    table_seq = normal_values(splits[20], (BUCKETS_SEQ, HEADS), 1.0, 6.0)
    table_x = normal_values(splits[21], (BUCKETS_BOX, HEADS), 1.0, 6.0)
    table_y = normal_values(splits[22], (BUCKETS_BOX, HEADS), 1.0, 6.0)
    out_grad = normal_values(splits[23], (TOKENS, D), 1.0, 6.0, ((0, 32),))
    return {"hidden_in": hidden_in, "doc_lengths": doc_lengths, "box_x": box_x, "box_y": box_y, "token_valid": token_valid, "w_query": w_query, "b_query": b_query, "w_key": w_key, "w_value": w_value, "b_value": b_value, "w_out": w_out, "b_out": b_out, "gain_attn": gain_attn, "shift_attn": shift_attn, "w_up": w_up, "b_up": b_up, "w_down": w_down, "b_down": b_down, "gain_out": gain_out, "shift_out": shift_out, "table_seq": table_seq, "table_x": table_x, "table_y": table_y, "out_grad": out_grad}


sequence_edges = (12, 16, 23, 32, 46, 64, 91)
edges_box = (20, 23, 27, 32, 39, 46, 54, 64, 77, 91, 108, 128, 153, 182, 216)
norm_eps = 1e-12
highest = lax.Precision.HIGHEST

@jax.custom_vjp
def low(v):
    return lax.optimization_barrier(v.astype(jnp.bfloat16)).astype(jnp.float32)

@jax.custom_vjp
def low_back(v):
    return v

def low_keep(v):
    return (low(v), None)

def low_pass(kept, grad):
    return (grad,)

def back_keep(v):
    return (v, None)

def back_low(kept, grad):
    return (low(grad),)
low.defvjp(low_keep, low_pass)
low_back.defvjp(back_keep, back_low)

def bucket_of(distance, near_span, edge_list, sign_offset):
    magnitude = jnp.abs(distance)
    bucket = jnp.minimum(magnitude, near_span)
    for edge_value in edge_list:
        bucket = bucket + (magnitude >= edge_value).astype(jnp.int32)
    return (bucket + jnp.where(distance > 0, sign_offset, 0)).astype(jnp.int32)

def layer_norm(value, gain, shift):
    center = value - lax.optimization_barrier(jnp.mean(value, axis=-1, keepdims=True))
    spread = lax.optimization_barrier(jnp.mean(center * center, axis=-1, keepdims=True))
    return center * lax.rsqrt(spread + norm_eps) * gain + shift

def layout(row_ids, doc_ends):
    forwarded_value = row_ids[:, None] >= doc_ends[None, :]
    doc_ids = lax.optimization_barrier(jnp.sum(forwarded_value.astype(jnp.int32), axis=1)).astype(jnp.int32)
    starts = lax.optimization_barrier(jnp.max(jnp.where(forwarded_value, doc_ends[None, :], 0), axis=1))
    offsets = row_ids - starts
    places = jnp.where(offsets < VISUAL, offsets, offsets - VISUAL)
    return (doc_ids, places.astype(jnp.int32))

def group_attention(query, key, value, tables, lengths, box_x, box_y, token_valid):
    count = box_x.shape[0]
    reach = TOK_DEV
    span = KEY_BLOCK + 2 * reach
    block_list = count // KEY_BLOCK
    doc_ends = jnp.cumsum(lengths).astype(jnp.int32)
    doc_ids, places = layout(jnp.arange(count, dtype=jnp.int32), doc_ends)
    table_seq, table_x, table_y = tables

    def widen(item, fill):
        edge = jnp.full((reach,) + item.shape[1:], fill, item.dtype)
        return jnp.concatenate([edge, item, edge], axis=0)
    key_wide = widen(key, 0.0)
    value_wide = widen(value, 0.0)
    doc_wide = widen(doc_ids, -1)
    place_wide = widen(places, 0)
    x_wide = widen(box_x, 0)
    y_wide = widen(box_y, 0)
    open_wide = widen((token_valid == 1).astype(jnp.int32), 0)

    def block(index):
        start = (index * KEY_BLOCK).astype(jnp.int32)
        query_block = lax.dynamic_slice_in_dim(query, start, KEY_BLOCK)
        doc_block = lax.dynamic_slice_in_dim(doc_ids, start, KEY_BLOCK)
        pos_block = lax.dynamic_slice_in_dim(places, start, KEY_BLOCK)
        x_block = lax.dynamic_slice_in_dim(box_x, start, KEY_BLOCK)
        y_block = lax.dynamic_slice_in_dim(box_y, start, KEY_BLOCK)
        key_block = lax.dynamic_slice_in_dim(key_wide, start, span)
        value_block = lax.dynamic_slice_in_dim(value_wide, start, span)
        key_docs = lax.dynamic_slice_in_dim(doc_wide, start, span)
        key_pos = lax.dynamic_slice_in_dim(place_wide, start, span)
        key_x = lax.dynamic_slice_in_dim(x_wide, start, span)
        key_y = lax.dynamic_slice_in_dim(y_wide, start, span)
        key_open = lax.dynamic_slice_in_dim(open_wide, start, span)
        raw = jnp.einsum('qhd,khd->hqk', query_block, key_block, precision=highest)
        bias = jnp.take(table_seq, bucket_of(key_pos[None, :] - pos_block[:, None], 8, sequence_edges, 16), axis=0)
        bias = bias + jnp.take(table_x, bucket_of(key_x[None, :] - x_block[:, None], 16, edges_box, 32), axis=0)
        bias = bias + jnp.take(table_y, bucket_of(key_y[None, :] - y_block[:, None], 16, edges_box, 32), axis=0)
        scores = low_back(raw + jnp.transpose(bias, (2, 0, 1)))
        allowed = (doc_block[:, None] == key_docs[None, :]) & (key_open[None, :] == 1)
        scores = jnp.where(allowed[None], scores, -jnp.inf)
        top = lax.optimization_barrier(jnp.max(scores, axis=-1, keepdims=True))
        weights = jnp.exp(scores - top)
        probs = weights / lax.optimization_barrier(jnp.sum(weights, axis=-1, keepdims=True))
        return jnp.einsum('hqk,khd->qhd', low(probs), value_block, precision=highest)
    result = lax.map(jax.checkpoint(block), jnp.arange(block_list, dtype=jnp.int32))
    return result.reshape(count, D)

def forward(inputs, w_query, b_query, w_key, w_value, b_value, w_out, b_out, gain_attn, shift_attn, w_up, b_up, w_down, b_down, gain_out, shift_out, table_seq, table_x, table_y, meta):
    doc_lengths, box_x, box_y, token_valid = meta
    query = low(low_back((jnp.dot(inputs, w_query, precision=highest) + b_query) * 0.125))
    key = low(low_back(jnp.dot(inputs, w_key, precision=highest)))
    value = low(low_back(jnp.dot(inputs, w_value, precision=highest) + b_value))
    count = TOK_DEV * N_FFN
    pieces = []
    for group in range(N_SEQ):
        rows = slice(group * count, (group + 1) * count)
        pieces.append(group_attention(query[rows].reshape(count, HEADS, HEAD_DIM), key[rows].reshape(count, HEADS, HEAD_DIM), value[rows].reshape(count, HEADS, HEAD_DIM), (table_seq, table_x, table_y), doc_lengths[group], box_x[rows], box_y[rows], token_valid[rows]))
    context = low(low_back(jnp.concatenate(pieces, axis=0)))
    attn = low_back(jnp.dot(context, w_out, precision=highest) + b_out)
    normed = layer_norm(inputs + attn, gain_attn, shift_attn)
    pre = low_back(jnp.dot(low(normed), w_up, precision=highest) + b_up)
    active = low(jax.nn.gelu(pre, approximate=False))
    branch = low_back(jnp.dot(active, w_down, precision=highest) + b_down)
    return layer_norm(normed + branch, gain_out, shift_out)

def reference(hidden_in, doc_lengths, box_x, box_y, token_valid, w_query, b_query, w_key, w_value, b_value, w_out, b_out, gain_attn, shift_attn, w_up, b_up, w_down, b_down, gain_out, shift_out, table_seq, table_x, table_y, out_grad):
    floats = [item.astype(jnp.float32) for item in (hidden_in, w_query, b_query, w_key, w_value, b_value, w_out, b_out, gain_attn, shift_attn, w_up, b_up, w_down, b_down, gain_out, shift_out, table_seq, table_x, table_y)]
    meta = (doc_lengths, box_x, box_y, token_valid)

    def wrapped(*values):
        return forward(*values, meta)
    output, pull = jax.vjp(wrapped, *floats)
    grads = pull(out_grad.astype(jnp.float32))
    return (output, grads[0], grads[1], grads[2], grads[3], grads[4], grads[5], grads[6], grads[7], grads[8], grads[9], grads[10], grads[11], grads[12], grads[13], grads[14], grads[15], grads[16], grads[17], grads[18])
```

```python
import functools

import jax
import jax.numpy as jnp
from jax import lax
from jax.experimental import pallas as pl
from jax.experimental.pallas import tpu as pltpu
from jax.sharding import PartitionSpec as P

VISUAL = 49
norm_eps = 1e-12
F32 = jnp.float32
BF16 = jnp.bfloat16
QB = 128
KB = 128
RB = 16
PAIRS = 6
NEG = -1e30
TILES = 12


def nn(a, b):
    return lax.dot_general(a, b, (((1,), (0,)), ((), ())), preferred_element_type=F32)


def nt(a, b):
    return lax.dot_general(a, b, (((1,), (1,)), ((), ())), preferred_element_type=F32)


def log_bucket(d, near, per_octave, sign):
    mag = jnp.abs(d)
    far = jnp.floor(jnp.log2(jnp.maximum(mag, 1.0) * (1.0 / near)) * per_octave + 0.0002) + near
    far = jnp.minimum(far, 2.0 * near - 1.0)
    return jnp.where(mag < near, mag, far) + jnp.where(d > 0, F32(sign), F32(0))


def put_buckets(b_ref, kmeta, qmeta, doc):
    key_doc = jnp.where(kmeta[:, 3:4] == doc.astype(F32), kmeta[:, 3:4], -1.0)
    same = key_doc == qmeta[3:4, :]
    b_ref[0] = jnp.where(same, log_bucket(kmeta[:, 0:1] - qmeta[0:1, :], 8.0, 2.0, 16.0), 16.0)
    b_ref[1] = log_bucket(kmeta[:, 1:2] - qmeta[1:2, :], 16.0, 4.0, 32.0)
    b_ref[2] = log_bucket(kmeta[:, 2:3] - qmeta[2:3, :], 16.0, 4.0, 32.0)


def one_hot(b_ref, row, count):
    cols = []
    for r in range(count):
        parts = []
        for t, size in ((0, 32), (1, 64), (2, 64)):
            v = jnp.broadcast_to(b_ref[t, pl.ds(row + r, 1), :], (size, QB)).astype(BF16)
            levels = lax.broadcasted_iota(jnp.int32, (size, QB), 0).astype(F32).astype(BF16)
            parts.append(jnp.where(v == levels, BF16(1), BF16(0)))
        cols.append(jnp.concatenate(parts, axis=0))
    return jnp.concatenate(cols, axis=1)


def fill_stack(stack, src):
    lane = lax.broadcasted_iota(jnp.int32, (QB, 128), 1)
    for p in range(PAIRS):
        x = src[:, 128 * p : 128 * p + 128].astype(F32)
        stack[p, 0:QB, :] = jnp.where(lane < 64, x, 0.0).astype(BF16)
        stack[p, QB : 2 * QB, :] = jnp.where(lane < 64, 0.0, x).astype(BF16)


def window_copies(pieces, keys, values, sems):
    rows = pieces[0].shape[0]
    return [
        pltpu.make_async_copy(piece, (keys, values)[i % 2].at[pl.ds(i // 2 * rows, rows), :], sems.at[i])
        for i, piece in enumerate(pieces)
    ]


def clear_tail(keys, values):
    for ref in (keys, values):
        ref[ref.shape[0] - KB :, :] = jnp.zeros((KB, ref.shape[1]), ref.dtype)


def tile_of(tiles, qb, t):
    return pl.multiple_of(tiles[qb, 1 + t], 16), tiles[qb, 1 + TILES + t]


def fwd_kernel(tiles, q_ref, k_low, v_low, k_own, v_own, k_high, v_high, kmeta_ref, qmeta_ref, tab_ref, ctx_ref, inv_ref, p_hbm,
               keys, values, s_scr, b_scr, bias_scr, qstack, ctx_t, m_scr, l_scr, pbuf, sems, in_sems):
    qb = pl.program_id(0)
    count = tiles[qb, 0]

    @pl.when(qb == 0)
    def _():
        copies = window_copies((k_low, v_low, k_own, v_own, k_high, v_high), keys, values, in_sems)
        for copy in copies:
            copy.start()
        clear_tail(keys, values)
        for copy in copies:
            copy.wait()

    fill_stack(qstack, q_ref)
    m_scr[...] = jnp.full_like(m_scr, -3e38)
    l_scr[...] = jnp.zeros_like(l_scr)
    ctx_t[...] = jnp.zeros_like(ctx_t)
    tab = tab_ref[...]

    def pass1(c, carry):
        base, doc = tile_of(tiles, qb, c)
        put_buckets(b_scr, kmeta_ref[pl.ds(base, KB), :], qmeta_ref[...], doc)

        def rows(g, carry):
            j = g * RB
            out = nn(tab, one_hot(b_scr, j, RB))
            for r in range(RB):
                bias_scr[pl.ds(j + r, 16, stride=KB), :] = out[:, r * QB : (r + 1) * QB]
            return carry

        lax.fori_loop(0, KB // RB, rows, 0, unroll=KB // RB)
        for p in range(PAIRS):
            raw = nt(keys[pl.ds(base, KB), 128 * p : 128 * p + 128], qstack[p])
            o = 8 + p
            s = raw + jnp.concatenate([bias_scr[p * KB : (p + 1) * KB, :], bias_scr[o * KB : (o + 1) * KB, :]], axis=1)
            s_scr[c, p] = s
            m_scr[p] = jnp.maximum(m_scr[p], jnp.max(s.reshape(KB // 8, 8, 2 * QB), axis=0))
        return carry

    lax.fori_loop(0, count, pass1, 0)
    for p in range(PAIRS):
        m_scr[p] = jnp.broadcast_to(jnp.max(m_scr[p], axis=0, keepdims=True), (8, 2 * QB))

    def pcopy(slot, c):
        return pltpu.make_async_copy(pbuf.at[slot], p_hbm.at[qb, c], sems.at[slot])

    def pass2(c, carry):
        base, _ = tile_of(tiles, qb, c)
        slot = lax.rem(c, 2)

        @pl.when(c >= 2)
        def _():
            pcopy(slot, c).wait()

        for p in range(PAIRS):
            e = jnp.exp(s_scr[c, p] - m_scr[p, 0:1, :])
            l_scr[p] = l_scr[p] + jnp.sum(e.reshape(KB // 8, 8, 2 * QB), axis=0)
            pb = e.astype(BF16)
            pbuf[slot, p] = pb
            value_t = values[pl.ds(base, KB), 128 * p : 128 * p + 128].T
            for h in range(2):
                r = 128 * p + 64 * h
                ctx_t[r : r + 64, :] = ctx_t[r : r + 64, :] + nn(value_t[64 * h : 64 * h + 64], pb[:, h * QB : (h + 1) * QB])
        pcopy(slot, c).start()
        return carry

    lax.fori_loop(0, count, pass2, 0)
    for p in range(PAIRS):
        inv = 1.0 / jnp.sum(l_scr[p], axis=0, keepdims=True)
        wide = jnp.concatenate([jnp.broadcast_to(inv[:, :QB], (64, QB)), jnp.broadcast_to(inv[:, QB:], (64, QB))], axis=0)
        w = slice(128 * p, 128 * p + 128)
        ctx_ref[:, w] = (ctx_t[w, :] * wide).T
        inv_ref[:, w] = wide.T

    @pl.when(count >= 2)
    def _():
        pcopy(lax.rem(count, 2), 0).wait()

    pcopy(lax.rem(count + 1, 2), 0).wait()


def attention_fwd(tiles, q, pieces, kmeta, qmeta, tab):
    rows, width = q.shape
    span = kmeta.shape[0]
    nq, nc = rows // QB, TILES
    vm = pltpu.VMEM
    hbm = pl.BlockSpec(memory_space=pl.ANY)
    full = lambda *s: pl.BlockSpec(s, lambda i, r: (0,) * len(s))
    block = pl.BlockSpec((QB, width), lambda i, r: (i, 0))
    return pl.pallas_call(
        fwd_kernel,
        grid_spec=pltpu.PrefetchScalarGridSpec(
            num_scalar_prefetch=1, grid=(nq,),
            in_specs=[block] + [hbm] * 6 + [full(span, 128), pl.BlockSpec((8, QB), lambda i, r: (0, i)), full(16, 160)],
            out_specs=[block, block, hbm],
            scratch_shapes=[
                vm((span, width), BF16), vm((span, width), BF16),
                vm((nc, PAIRS, KB, 2 * QB), F32), vm((3, KB, QB), F32), vm((16 * KB, QB), F32),
                vm((PAIRS, 2 * QB, 128), BF16), vm((width, QB), F32), vm((PAIRS, 8, 2 * QB), F32),
                vm((PAIRS, 8, 2 * QB), F32), vm((2, PAIRS, KB, 2 * QB), BF16),
                pltpu.SemaphoreType.DMA((2,)), pltpu.SemaphoreType.DMA((6,))]),
        out_shape=[jax.ShapeDtypeStruct((rows, width), F32), jax.ShapeDtypeStruct((rows, width), F32),
                   jax.ShapeDtypeStruct((nq, nc, PAIRS, KB, 2 * QB), BF16)],
        compiler_params=pltpu.CompilerParams(vmem_limit_bytes=56 * 2**20, dimension_semantics=("arbitrary",)),
        cost_estimate=pl.CostEstimate(flops=25 * 10**9, bytes_accessed=30 * 2**20, transcendentals=5 * 10**6),
        name="attention_forward",
    )(tiles, q, *pieces, kmeta, qmeta, tab)


def order_tables(ts, tx, ty):
    t = jnp.concatenate([ts.at[16].set(NEG), tx, ty], axis=0).T
    z = jnp.zeros((2, 160), t.dtype)
    return jnp.concatenate([t[0::2], z, t[1::2], z], axis=0)


def bwd_kernel(tiles, q_ref, dc_ref, ctx_ref, k_low, v_low, k_own, v_own, k_high, v_high, kmeta_ref, qmeta_ref, p_hbm,
               dq_ref, low_ref, own_k, own_v, high_ref, dtab_ref,
               keys, values, dk, dv, dq_t, b_scr, ds_scr, delta, qstack, cstack, pbuf, sems, in_sems):
    qb = pl.program_id(0)
    last = pl.num_programs(0) - 1
    count = tiles[qb, 0]

    def pcopy(c):
        slot = lax.rem(c, 2)
        return pltpu.make_async_copy(p_hbm.at[qb, c], pbuf.at[slot], sems.at[slot])

    pcopy(0).start()

    @pl.when(qb == 0)
    def _():
        copies = window_copies((k_low, v_low, k_own, v_own, k_high, v_high), keys, values, in_sems)
        for copy in copies:
            copy.start()
        clear_tail(keys, values)
        dk[...] = jnp.zeros_like(dk)
        dv[...] = jnp.zeros_like(dv)
        dtab_ref[...] = jnp.zeros_like(dtab_ref)
        ds_scr[...] = jnp.zeros_like(ds_scr)
        for copy in copies:
            copy.wait()

    fill_stack(qstack, q_ref)
    fill_stack(cstack, dc_ref)
    for p in range(PAIRS):
        w = slice(128 * p, 128 * p + 128)
        both = (dc_ref[:, w].astype(F32) * ctx_ref[:, w]).T
        delta[p : p + 1, :] = jnp.concatenate(
            [jnp.sum(both[:64], axis=0, keepdims=True), jnp.sum(both[64:], axis=0, keepdims=True)], axis=1)
    dq_t[...] = jnp.zeros_like(dq_t)

    def tile(c, carry):
        base, doc = tile_of(tiles, qb, c)
        slot = lax.rem(c, 2)
        put_buckets(b_scr, kmeta_ref[pl.ds(base, KB), :], qmeta_ref[...], doc)

        @pl.when(c + 1 < count)
        def _():
            pcopy(c + 1).start()

        pcopy(c).wait()
        for p in range(PAIRS):
            w = slice(128 * p, 128 * p + 128)
            dp = nt(values[pl.ds(base, KB), w], cstack[p])
            pb = pbuf[slot, p]
            ds = pb.astype(F32) * (dp - delta[p : p + 1, :])
            ds_scr[p * KB : (p + 1) * KB, :] = ds[:, :QB]
            ds_scr[(8 + p) * KB : (9 + p) * KB, :] = ds[:, QB:]
            dsb = ds.astype(BF16)
            dk[pl.ds(base, KB), w] = dk[pl.ds(base, KB), w] + nn(dsb, qstack[p])
            dv[pl.ds(base, KB), w] = dv[pl.ds(base, KB), w] + nn(pb, cstack[p])
            key_t = keys[pl.ds(base, KB), w].T
            for h in range(2):
                r = 128 * p + 64 * h
                dq_t[r : r + 64, :] = dq_t[r : r + 64, :] + nn(key_t[64 * h : 64 * h + 64], dsb[:, h * QB : (h + 1) * QB])

        def rows(g, acc):
            j = g * RB
            d = jnp.concatenate([ds_scr[pl.ds(j + r, 16, stride=KB), :] for r in range(RB)], axis=1).astype(BF16)
            return acc + nt(d, one_hot(b_scr, j, RB))

        dtab_ref[...] = lax.fori_loop(0, KB // RB, rows, dtab_ref[...], unroll=KB // RB)
        return carry

    lax.fori_loop(0, count, tile, 0)
    for p in range(PAIRS):
        w = slice(128 * p, 128 * p + 128)
        dq_ref[:, w] = dq_t[w, :].T.astype(BF16)

    @pl.when(qb == last)
    def _():
        rows = own_k.shape[0]
        width = dk.shape[1]
        own = [
            pltpu.make_async_copy(dk.at[pl.ds(rows, rows), :], own_k, in_sems.at[0]),
            pltpu.make_async_copy(dv.at[pl.ds(rows, rows), :], own_v, in_sems.at[1]),
        ]
        for copy in own:
            copy.start()

        def move(i, carry):
            r = pl.multiple_of(i * 32, 32)
            for src, col in ((dk, 0), (dv, width)):
                low_ref[pl.ds(r, 32), col : col + width] = src[pl.ds(r, 32), :].astype(BF16)
                high_ref[pl.ds(r, 32), col : col + width] = src[pl.ds(pl.multiple_of(2 * rows + r, 32), 32), :].astype(BF16)
            return carry

        lax.fori_loop(0, rows // 32, move, 0)
        for copy in own:
            copy.wait()


def attention_bwd(tiles, q, dc, ctx, pieces, kmeta, qmeta, probs):
    rows, width = q.shape
    span = kmeta.shape[0]
    nq, nc = rows // QB, TILES
    vm = pltpu.VMEM
    hbm = pl.BlockSpec(memory_space=pl.ANY)
    full = lambda *s: pl.BlockSpec(s, lambda i, r: (0,) * len(s))
    block = pl.BlockSpec((QB, width), lambda i, r: (i, 0))
    shape = jax.ShapeDtypeStruct
    return pl.pallas_call(
        bwd_kernel,
        grid_spec=pltpu.PrefetchScalarGridSpec(
            num_scalar_prefetch=1, grid=(nq,),
            in_specs=[block] * 3 + [hbm] * 6 + [full(span, 128), pl.BlockSpec((8, QB), lambda i, r: (0, i)), hbm],
            out_specs=[block, full(rows, 2 * width), hbm, hbm, full(rows, 2 * width), full(16, 160)],
            scratch_shapes=[
                vm((span, width), BF16), vm((span, width), BF16),
                vm((span, width), F32), vm((span, width), F32), vm((width, QB), F32),
                vm((3, KB, QB), F32), vm((16 * KB, QB), F32), vm((8, 2 * QB), F32),
                vm((PAIRS, 2 * QB, 128), BF16), vm((PAIRS, 2 * QB, 128), BF16),
                vm((2, PAIRS, KB, 2 * QB), BF16), pltpu.SemaphoreType.DMA((2,)), pltpu.SemaphoreType.DMA((6,))]),
        out_shape=[shape((rows, width), BF16), shape((rows, 2 * width), BF16), shape((rows, width), F32), shape((rows, width), F32),
                   shape((rows, 2 * width), BF16), shape((16, 160), F32)],
        compiler_params=pltpu.CompilerParams(vmem_limit_bytes=56 * 2**20, dimension_semantics=("arbitrary",)),
        cost_estimate=pl.CostEstimate(flops=40 * 10**9, bytes_accessed=40 * 2**20, transcendentals=0),
        name="attention_backward",
    )(tiles, q, dc, ctx, *pieces, kmeta, qmeta, probs)


def exchange_plan(n_seq, n_ffn, half):
    seq_bits = [("seq", 1 << b) for b in range(n_seq.bit_length() - 1)]
    ffn_bits = [("ffn", 1 << b) for b in range(1, n_ffn.bit_length() - 1)]
    unit = 16 * n_seq * n_ffn // 2
    if half % (3 * unit) == 0:
        orders = [seq_bits + ffn_bits, ffn_bits + seq_bits, ffn_bits[1:] + seq_bits + ffn_bits[:1]]
        return orders, half // 3
    return [seq_bits + ffn_bits], half


def sum_kernel(orders, length, a_ref, small_ref, unit_ref, out_ref, small_out, unit_out, work, core_in, slots, sums, small_in,
               core_sems, core_back, send_sems, recv_sems, back_send, back_recv, small_send, small_recv, unit_in, unit_mid, unit_send, unit_recv):
    seq, ffn = lax.axis_index("seq"), lax.axis_index("ffn")
    half = work.shape[0]
    streams = len(orders)
    steps = len(orders[0])
    core = lax.rem(ffn, 2)

    def bit_of(axis, bit):
        return lax.rem((seq if axis == "seq" else ffn) // bit, 2)

    def partner(axis, bit):
        flip = bit * (1 - 2 * bit_of(axis, bit))
        return {axis: (seq if axis == "seq" else ffn) + flip}

    peers = [("ffn", 1)] + sorted(orders[0])
    barrier = pltpu.get_barrier_semaphore()
    for axis, bit in peers:
        pl.semaphore_signal(barrier, inc=1, device_id=partner(axis, bit), device_id_type=pl.DeviceIdType.MESH)
    pl.semaphore_wait(barrier, len(peers))

    def remote(src, dst, send, recv, axis, bit):
        return pltpu.make_async_remote_copy(src_ref=src, dst_ref=dst, send_sem=send, recv_sem=recv,
                                            device_id=partner(axis, bit), device_id_type=pl.DeviceIdType.MESH)

    def at(ref, start, size):
        return ref.at[pl.ds(start if isinstance(start, int) else pl.multiple_of(start, 16), size), :]

    def add(dst, dst_lo, one, one_lo, two, two_lo, size):
        def body(i, carry):
            r = i * 16
            dst[pl.ds(pl.multiple_of(dst_lo + r, 16), 16), :] = (
                one[pl.ds(pl.multiple_of(one_lo + r, 16), 16), :].astype(F32)
                + two[pl.ds(pl.multiple_of(two_lo + r, 16), 16), :].astype(F32)
            ).astype(BF16)
            return carry
        lax.fori_loop(0, size // 16, body, 0)

    pending = []
    firsts = []
    for s in range(streams):
        copy = remote(at(a_ref, (1 - core) * half + s * length, length), at(core_in, s * length, length),
                      core_sems.at[s], core_sems.at[streams + s], "ffn", 1)
        copy.start()
        firsts.append(copy)
    sums[0] = small_ref[...]

    def small_copy(k):
        axis, bit = peers[k]
        return remote(sums.at[k], small_in.at[k], small_send.at[k], small_recv.at[k], axis, bit)
    small_copy(0).start()
    seq_peers = [peer for peer in peers if peer[0] == "seq"]

    def unit_copy(k):
        src = unit_ref if k == 0 else unit_mid.at[k - 1]
        return remote(src, unit_in.at[k], unit_send.at[k], unit_recv.at[k], *seq_peers[k])

    def unit_step(k):
        unit_copy(k).wait_recv()

        def body(i, carry):
            rows = pl.ds(pl.multiple_of(i * 16, 16), 16)
            src = unit_ref[rows, :] if k == 0 else unit_mid[k - 1, rows, :]
            total = src.astype(F32) + unit_in[k, rows, :].astype(F32)
            if k == len(seq_peers) - 1:
                unit_out[rows, :] = total
            else:
                unit_mid[k, rows, :] = total.astype(BF16)
            return carry
        lax.fori_loop(0, unit_ref.shape[0] // 16, body, 0)
        if k < len(seq_peers) - 1:
            unit_copy(k + 1).start()

    lows = [s * length for s in range(streams)]
    sizes = [length] * streams
    offs = []
    base = 0
    for s in range(streams):
        own = []
        size = length
        for k in range(steps):
            size //= 2
            own.append((base, size))
            base += size
        offs.append(own)

    def scatter(s, k):
        axis, bit = orders[s][k]
        size = sizes[s] // 2
        mine = lows[s] + bit_of(axis, bit) * size
        theirs = lows[s] + (1 - bit_of(axis, bit)) * size
        slot, _ = offs[s][k]
        copy = remote(at(work, theirs, size), at(slots, slot, size), send_sems.at[s, k], recv_sems.at[s, k], axis, bit)
        copy.start()
        return copy, mine, size

    flying = []
    for s in range(streams):
        firsts[s].wait_recv()
        add(work, s * length, a_ref, core * half + s * length, core_in, s * length, length)
        flying.append(scatter(s, 0))
    for k in range(steps):
        for s in range(streams):
            copy, mine, size = flying[s]
            copy.wait_recv()
            slot, _ = offs[s][k]
            last = k == steps - 1
            if last:
                add(out_ref, core * half + mine, work, mine, slots, slot, size)
            else:
                add(work, mine, work, mine, slots, slot, size)
            pending.append(copy)
            lows[s], sizes[s] = mine, size
            if not last:
                flying[s] = scatter(s, k + 1)
            else:
                flying[s] = gather(s, k, lows, sizes, orders, remote, at, out_ref, core, half, back_send, back_recv)
        if k == 0:
            unit_copy(0).start()
        elif k <= len(seq_peers):
            unit_step(k - 1)
        small_copy(k).wait_recv()
        sums[k + 1] = sums[k] + small_in[k]
        small_copy(k + 1).start()
    small_copy(steps).wait_recv()
    small_out[...] = sums[steps] + small_in[steps]
    finals = []
    for k in range(steps - 1, -1, -1):
        for s in range(streams):
            copy = flying[s]
            copy.wait_recv()
            pending.append(copy)
            axis, bit = orders[s][k]
            lows[s] = lows[s] - bit_of(axis, bit) * sizes[s]
            sizes[s] = 2 * sizes[s]
            if k:
                flying[s] = gather(s, k - 1, lows, sizes, orders, remote, at, out_ref, core, half, back_send, back_recv)
            else:
                copy = remote(at(out_ref, core * half + s * length, length), at(out_ref, core * half + s * length, length),
                              core_back.at[s], core_back.at[streams + s], "ffn", 1)
                copy.start()
                finals.append(copy)
    for copy in finals:
        copy.wait_recv()
    for copy in firsts + pending + finals:
        copy.wait_send()
    for k in range(steps + 1):
        small_copy(k).wait_send()
    for k in range(len(seq_peers)):
        unit_copy(k).wait_send()


def gather(s, k, lows, sizes, orders, remote, at, out_ref, core, half, back_send, back_recv):
    axis, bit = orders[s][k]
    place = at(out_ref, core * half + lows[s], sizes[s])
    copy = remote(place, place, back_send.at[s, k], back_recv.at[s, k], axis, bit)
    copy.start()
    return copy


def sum_everywhere(a, small, unit):
    n_seq, n_ffn = lax.axis_size("seq"), lax.axis_size("ffn")
    grain = 16 * n_seq * n_ffn // 2
    rows, width = a.shape
    half = -(-(rows // 2) // grain) * grain
    if 2 * half > rows:
        a = jnp.pad(a, ((0, 2 * half - rows), (0, 0)))
    orders, length = exchange_plan(n_seq, n_ffn, half)
    streams, steps = len(orders), len(orders[0])
    vm, dma = pltpu.VMEM, pltpu.SemaphoreType.DMA
    slot_rows = streams * (length - length // (1 << steps))
    bits = n_seq.bit_length() - 1
    out, small_out, unit_out = pl.pallas_call(
        functools.partial(sum_kernel, orders, length),
        out_shape=[jax.ShapeDtypeStruct(a.shape, BF16), jax.ShapeDtypeStruct(small.shape, F32), jax.ShapeDtypeStruct(unit.shape, F32)],
        in_specs=[pl.BlockSpec(memory_space=vm)] * 3,
        out_specs=[pl.BlockSpec(memory_space=vm)] * 3,
        scratch_shapes=[
            vm((half, width), BF16), vm((half, width), BF16), vm((slot_rows, width), BF16),
            vm((steps + 1,) + small.shape, F32), vm((steps + 1,) + small.shape, F32),
            dma((2 * streams,)), dma((2 * streams,)), dma((streams, steps)), dma((streams, steps)),
            dma((streams, steps)), dma((streams, steps)), dma((steps + 1,)), dma((steps + 1,)),
            vm((bits,) + unit.shape, BF16), vm((bits,) + unit.shape, BF16), dma((bits,)), dma((bits,)),
        ],
        compiler_params=pltpu.CompilerParams(collective_id=0, has_side_effects=True, vmem_limit_bytes=48 * 2**20),
        name="sum_everywhere",
    )(a, small, unit)
    return out[:rows], small_out, unit_out


UB = 512


def gelu_and_slope(x):
    z = jnp.abs(x) * 0.7071067811865476
    t = 1.0 / (1.0 + 0.3275911 * z)
    poly = ((((1.061405429 * t - 1.453152027) * t + 1.421413741) * t - 0.284496736) * t + 0.254829592) * t
    bell = jnp.exp(-z * z)
    tail = 0.5 * poly * bell
    phi = jnp.where(x < 0, tail, 1.0 - tail)
    return x * phi, phi + x * bell * 0.3989422804014327


def tn(a, b):
    return lax.dot_general(a, b, (((0,), (0,)), ((), ())), preferred_element_type=F32)


def ffn_up_kernel(normed_ref, up_ref, down_ref, active_ref, slope_ref, branch_ref):
    @pl.when(pl.program_id(0) == 0)
    def _():
        branch_ref[...] = jnp.zeros_like(branch_ref)

    rows = normed_ref.shape[0]
    size = rows // 2
    for r in range(0, rows, size):
        w = slice(r, r + size)
        act, slope = gelu_and_slope(nt(normed_ref[w, :], up_ref[...]))
        act = act.astype(BF16)
        active_ref[w, :] = act
        slope_ref[w, :] = slope.astype(BF16)
        branch_ref[w, :] = branch_ref[w, :] + nn(act, down_ref[...])


def ffn_up(normed, up, down):
    rows, wide = normed.shape
    units, width = down.shape
    full = lambda *s: pl.BlockSpec(s, lambda i: (0,) * len(s))
    col = pl.BlockSpec((rows, UB), lambda i: (0, i))
    shape = jax.ShapeDtypeStruct
    return pl.pallas_call(
        ffn_up_kernel,
        grid=(units // UB,),
        in_specs=[full(rows, wide), pl.BlockSpec((UB, wide), lambda i: (i, 0)), pl.BlockSpec((UB, width), lambda i: (i, 0))],
        out_specs=[col, col, full(rows, width)],
        out_shape=[shape((rows, units), BF16), shape((rows, units), BF16), shape((rows, width), F32)],
        compiler_params=pltpu.CompilerParams(vmem_limit_bytes=48 * 2**20, dimension_semantics=("arbitrary",)),
        cost_estimate=pl.CostEstimate(flops=2 * rows * units * (wide + width), bytes_accessed=20 * 2**20, transcendentals=2 * rows * units),
        name="ffn_up",
    )(normed, up, down)


def ffn_back_kernel(grad_ref, normed_ref, up_ref, down_ref, active_ref, slope_ref, unit_ref, normed_grad_ref):
    @pl.when(pl.program_id(0) == 0)
    def _():
        normed_grad_ref[...] = jnp.zeros_like(normed_grad_ref)

    grad = grad_ref[...]
    wide = normed_ref.shape[1]
    width = grad.shape[1]
    unit_ref[:, wide:] = tn(active_ref[...], grad).astype(BF16)
    pre = (nt(grad, down_ref[...]) * slope_ref[...].astype(F32)).astype(BF16)
    unit_ref[:, :wide] = tn(pre, normed_ref[...]).astype(BF16)
    normed_grad_ref[...] = normed_grad_ref[...] + nn(pre, up_ref[:, :width])


def ffn_back(grad, normed, up, down, active, slope):
    rows, wide = normed.shape
    units, width = down.shape
    full = lambda *s: pl.BlockSpec(s, lambda i: (0,) * len(s))
    col = pl.BlockSpec((rows, UB), lambda i: (0, i))
    row = lambda n: pl.BlockSpec((UB, n), lambda i: (i, 0))
    shape = jax.ShapeDtypeStruct
    return pl.pallas_call(
        ffn_back_kernel,
        grid=(units // UB,),
        in_specs=[full(rows, width), full(rows, wide), row(wide), row(width), col, col],
        out_specs=[row(wide + width), full(rows, width)],
        out_shape=[shape((units, wide + width), BF16), shape((rows, width), F32)],
        compiler_params=pltpu.CompilerParams(vmem_limit_bytes=48 * 2**20, dimension_semantics=("arbitrary",)),
        cost_estimate=pl.CostEstimate(flops=4 * rows * units * (wide + width), bytes_accessed=30 * 2**20, transcendentals=0),
        name="ffn_back",
    )(grad, normed, up, down, active, slope)


def from_behind(x, axis, by):
    devices = lax.axis_size(axis)
    pairs = [(i, i + by) for i in range(devices) if 0 <= i + by < devices]
    return lax.ppermute(x, axis, pairs)


def layer_norm(value, gain, shift):
    center = value - jnp.mean(value, axis=-1, keepdims=True)
    spread = jnp.mean(center * center, axis=-1, keepdims=True)
    return center * lax.rsqrt(spread + norm_eps) * gain + shift


def layout(row_ids, doc_ends):
    forwarded_value = row_ids[:, None] >= doc_ends[None, :]
    doc_ids = jnp.sum(forwarded_value.astype(jnp.int32), axis=1)
    starts = jnp.max(jnp.where(forwarded_value, doc_ends[None, :], 0), axis=1)
    offsets = row_ids - starts
    places = jnp.where(offsets < VISUAL, offsets, offsets - VISUAL)
    return (doc_ids, places)


def tile_table(starts, doc_ids, key_docs, window_start, rows):
    docs = jnp.arange(starts.shape[0] - 1, dtype=jnp.int32)
    place = jnp.arange(doc_ids.shape[0], dtype=jnp.int32)
    ends = jnp.max(jnp.where(key_docs[None, :] == docs[:, None], place[None, :] + 1, 0), axis=1)
    own = doc_ids[rows : 2 * rows]
    segments = own[0::QB, None] + jnp.arange(3, dtype=jnp.int32)[None, :]
    active = segments <= own[QB - 1 :: QB, None]
    hit = segments[:, :, None] == docs[None, None, :]
    low = jnp.sum(jnp.where(hit, starts[None, None, :-1], 0), axis=2) - window_start
    low = jnp.maximum(low, 0) // 16 * 16
    high = jnp.sum(jnp.where(hit, ends[None, None, :], 0), axis=2)
    count = jnp.where(active, jnp.maximum(high - low + KB - 1, 0) // KB, 0)
    before = jnp.cumsum(count, axis=1) - count
    index = jnp.arange(TILES, dtype=jnp.int32)[None, None, :] - before[:, :, None]
    inside = (index >= 0) & (index < count[:, :, None])
    base = jnp.sum(jnp.where(inside, low[:, :, None] + KB * index, 0), axis=1)
    doc = jnp.sum(jnp.where(inside, segments[:, :, None], 0), axis=1)
    return jnp.concatenate([jnp.sum(count, axis=1, keepdims=True), base, doc], axis=1).astype(jnp.int32)


def on_device(
    hidden_in, doc_lengths, box_x, box_y, token_valid, w_query, b_query, w_key, w_value, b_value,
    w_out, b_out, gain_attn, shift_attn, w_up, b_up, w_down, b_down, gain_out, shift_out,
    table_seq, table_x, table_y, out_grad,
):
    rows = hidden_in.shape[0]
    width = hidden_in.shape[1]
    heads = table_seq.shape[1]
    group_rows = box_x.shape[0]
    span = 3 * rows
    first_row = lax.axis_index("ffn") * rows
    doc_ends = jnp.cumsum(doc_lengths[0])

    n_ffn = lax.axis_size("ffn")
    up = [(i, i + 1) for i in range(n_ffn - 1)]
    hidden_low = lax.ppermute(hidden_in, "ffn", up)
    hidden_high = lax.ppermute(hidden_in, "ffn", [(j, i) for i, j in up])

    units = b_up.shape[0]
    up_ext = jnp.concatenate([w_up.T, b_up[:, None], jnp.zeros((units, 127), BF16)], axis=1)
    up_all = lax.all_gather(up_ext, "ffn", axis=0, tiled=True)
    down_all = lax.all_gather(w_down, "ffn", axis=0, tiled=True)

    window_rows = first_row - rows + jnp.arange(span, dtype=jnp.int32)
    doc_ids, places = layout(window_rows, doc_ends)
    inside = (window_rows >= 0) & (window_rows < group_rows)

    def window_of(item):
        edge = jnp.zeros((rows,), item.dtype)
        padded = jnp.concatenate([edge, item, edge])
        return lax.dynamic_slice_in_dim(padded, first_row, span)

    win_x, win_y = window_of(box_x), window_of(box_y)
    key_open = (window_of(token_valid) == 1) & inside
    key_docs = jnp.where(key_open, doc_ids, -1)
    kmeta = jnp.stack([places, win_x, win_y, key_docs], axis=1).astype(F32)
    kmeta = jnp.pad(kmeta, ((0, KB), (0, 124)), constant_values=-1.0)
    own = slice(rows, 2 * rows)
    qmeta = jnp.stack([places[own], win_x[own], win_y[own], doc_ids[own]], axis=0).astype(F32)
    qmeta = jnp.pad(qmeta, ((0, 4), (0, 0)))
    starts = jnp.concatenate([jnp.zeros((1,), doc_ends.dtype), doc_ends])
    tiles = tile_table(starts, doc_ids, key_docs, first_row - rows, rows)
    tables = order_tables(table_seq, table_x, table_y)

    query = ((jnp.dot(hidden_in, w_query, preferred_element_type=F32) + b_query) * 0.125).astype(BF16)
    pieces = []
    for part in (hidden_low, hidden_in, hidden_high):
        pieces.append(jnp.dot(part, w_key, preferred_element_type=F32).astype(BF16))
        pieces.append((jnp.dot(part, w_value, preferred_element_type=F32) + b_value).astype(BF16))

    context, inv, probs = attention_fwd(tiles, query, pieces, kmeta, qmeta, tables)
    context_low = context.astype(BF16)
    attn = jnp.dot(context_low, w_out, preferred_element_type=F32) + b_out
    inputs = hidden_in.astype(F32)
    normed, norm_pull = jax.vjp(
        layer_norm, inputs + attn, gain_attn.astype(F32), shift_attn.astype(F32)
    )
    normed_low = normed.astype(BF16)
    ones = jnp.concatenate([jnp.ones((rows, 1), BF16), jnp.zeros((rows, 127), BF16)], axis=1)
    normed_ext = jnp.concatenate([normed_low, ones], axis=1)
    active, slope, branch = ffn_up(normed_ext, up_all, down_all)
    hidden_out, out_pull = jax.vjp(
        layer_norm, normed + (branch + b_down), gain_out.astype(F32), shift_out.astype(F32)
    )
    mid_grad, grad_gain_out, grad_shift_out = out_pull(out_grad.astype(F32))
    branch_grad = mid_grad.astype(BF16)
    grad_b_down = jnp.sum(branch_grad.astype(F32), axis=0)
    unit_part, branch_back = ffn_back(branch_grad, normed_ext, up_all, down_all, active, slope)
    unit_grad = lax.psum_scatter(unit_part, "ffn", scatter_dimension=0, tiled=True)
    normed_grad = mid_grad + branch_back
    mid1_grad, grad_gain_attn, grad_shift_attn = norm_pull(normed_grad)
    attn_grad = mid1_grad.astype(BF16)
    grad_b_out = jnp.sum(attn_grad.astype(F32), axis=0)
    grad_w_out = jnp.dot(context_low.T, attn_grad, preferred_element_type=F32)
    scaled = (nt(attn_grad, w_out) * inv).astype(BF16)
    query_grad, low_terms, own_key, own_value, high_terms, table_sum = attention_bwd(
        tiles, query, scaled, context, pieces, kmeta, qmeta, probs
    )
    from_below = from_behind(high_terms, "ffn", 1).astype(F32)
    from_above = from_behind(low_terms, "ffn", -1).astype(F32)
    key_grad = (own_key + from_below[:, :width] + from_above[:, :width]).astype(BF16)
    value_grad = (own_value + from_below[:, width:] + from_above[:, width:]).astype(BF16)
    hidden_grad = (
        mid1_grad + nt(query_grad, w_query) * 0.125 + nt(key_grad, w_key) + nt(value_grad, w_value)
    )
    big = jnp.concatenate(
        [
            (jnp.dot(hidden_in.T, query_grad, preferred_element_type=F32) * 0.125).astype(BF16),
            jnp.dot(hidden_in.T, key_grad, preferred_element_type=F32).astype(BF16),
            jnp.dot(hidden_in.T, value_grad, preferred_element_type=F32).astype(BF16),
            grad_w_out.astype(BF16),
        ],
        axis=0,
    )
    small = jnp.stack(
        [
            jnp.sum(query_grad.astype(F32), axis=0) * 0.125,
            jnp.sum(value_grad.astype(F32), axis=0),
            grad_b_out,
            grad_gain_attn,
            grad_shift_attn,
            grad_b_down,
            grad_gain_out,
            grad_shift_out,
        ]
    )
    levels = table_sum.shape[1]
    small = jnp.concatenate([small, jnp.pad(table_sum, ((0, 0), (0, width - levels)))], axis=0)
    big, small, unit_grad = sum_everywhere(big, small, unit_grad)
    grad_w_up = unit_grad[:, :width].T
    grad_b_up = unit_grad[:, width]
    grad_w_down = unit_grad[:, width + 128 :]
    grads = [big[i * width : (i + 1) * width].astype(F32) for i in range(4)]
    vec = [small[i] for i in range(8)]
    table_all = jnp.stack([small[8 + h // 2 + 8 * (h % 2), :levels] for h in range(heads)], axis=1)
    return (
        hidden_out, hidden_grad, grads[0], vec[0], grads[1], grads[2], vec[1], grads[3], vec[2], vec[3], vec[4],
        grad_w_up, grad_b_up, grad_w_down, vec[5], vec[6], vec[7],
        table_all[:32], table_all[32:96], table_all[96:],
    )


def solution(mesh):
    in_specs = (
        P(("seq", "ffn"), None),
        P("seq", None),
        P("seq"),
        P("seq"),
        P("seq"),
        P(),
        P(),
        P(),
        P(),
        P(),
        P(),
        P(),
        P(),
        P(),
        P(None, "ffn"),
        P("ffn"),
        P("ffn", None),
        P(),
        P(),
        P(),
        P(),
        P(),
        P(),
        P(("seq", "ffn"), None),
    )
    out_specs = (
        P(("seq", "ffn"), None),
        P(("seq", "ffn"), None),
        P(),
        P(),
        P(),
        P(),
        P(),
        P(),
        P(),
        P(),
        P(),
        P(None, "ffn"),
        P("ffn"),
        P("ffn", None),
        P(),
        P(),
        P(),
        P(),
        P(),
        P(),
    )
    return jax.shard_map(
        on_device, mesh=mesh, in_specs=in_specs, out_specs=out_specs, check_vma=False
    )
```

```python
import functools

import jax
import jax.numpy as jnp
from jax import lax
from jax.experimental import pallas as pl
from jax.experimental.pallas import tpu as pltpu
from jax.sharding import PartitionSpec as P

VISUAL = 49
norm_eps = 1e-12
F32 = jnp.float32
BF16 = jnp.bfloat16
QB = 128
KB = 128
RB = 16
PAIRS = 6
NEG = -1e30
TILES = 12


def nn(a, b):
    return lax.dot_general(a, b, (((1,), (0,)), ((), ())), preferred_element_type=F32)


def nt(a, b):
    return lax.dot_general(a, b, (((1,), (1,)), ((), ())), preferred_element_type=F32)


def log_bucket(d, near, per_octave, sign):
    mag = jnp.abs(d)
    far = jnp.floor(jnp.log2(jnp.maximum(mag, 1.0) * (1.0 / near)) * per_octave + 0.0002) + near
    far = jnp.minimum(far, 2.0 * near - 1.0)
    return jnp.where(mag < near, mag, far) + jnp.where(d > 0, F32(sign), F32(0))


def put_buckets(b_ref, kmeta, qmeta, doc):
    key_doc = jnp.where(kmeta[:, 3:4] == doc.astype(F32), kmeta[:, 3:4], -1.0)
    same = key_doc == qmeta[3:4, :]
    b_ref[0] = jnp.where(same, log_bucket(kmeta[:, 0:1] - qmeta[0:1, :], 8.0, 2.0, 16.0), 16.0)
    b_ref[1] = log_bucket(kmeta[:, 1:2] - qmeta[1:2, :], 16.0, 4.0, 32.0)
    b_ref[2] = log_bucket(kmeta[:, 2:3] - qmeta[2:3, :], 16.0, 4.0, 32.0)


def one_hot(b_ref, row, count):
    cols = []
    for r in range(count):
        parts = []
        for t, size in ((0, 32), (1, 64), (2, 64)):
            v = jnp.broadcast_to(b_ref[t, pl.ds(row + r, 1), :], (size, QB)).astype(BF16)
            levels = lax.broadcasted_iota(jnp.int32, (size, QB), 0).astype(F32).astype(BF16)
            parts.append(jnp.where(v == levels, BF16(1), BF16(0)))
        cols.append(jnp.concatenate(parts, axis=0))
    return jnp.concatenate(cols, axis=1)


def fill_stack(stack, src):
    lane = lax.broadcasted_iota(jnp.int32, (QB, 128), 1)
    for p in range(PAIRS):
        x = src[:, 128 * p : 128 * p + 128].astype(F32)
        stack[p, 0:QB, :] = jnp.where(lane < 64, x, 0.0).astype(BF16)
        stack[p, QB : 2 * QB, :] = jnp.where(lane < 64, 0.0, x).astype(BF16)


def window_copies(k_hbm, v_hbm, keys, values, sems):
    rows = k_hbm.shape[0]
    return [
        pltpu.make_async_copy(k_hbm, keys.at[pl.ds(0, rows), :], sems.at[0]),
        pltpu.make_async_copy(v_hbm, values.at[pl.ds(0, rows), :], sems.at[1]),
    ]


def clear_tail(keys, values):
    for ref in (keys, values):
        ref[ref.shape[0] - KB :, :] = jnp.zeros((KB, ref.shape[1]), ref.dtype)


def tile_of(tiles, qb, t):
    return pl.multiple_of(tiles[qb, 1 + t], 16), tiles[qb, 1 + TILES + t]


def fwd_kernel(tiles, q_ref, k_hbm, v_hbm, kmeta_ref, qmeta_ref, tab_ref, ctx_ref, inv_ref, p_hbm,
               keys, values, s_scr, b_scr, bias_scr, qstack, ctx_t, m_scr, l_scr, pbuf, sems, in_sems):
    qb = pl.program_id(0)
    count = tiles[qb, 0]

    @pl.when(qb == 0)
    def _():
        copies = window_copies(k_hbm, v_hbm, keys, values, in_sems)
        for copy in copies:
            copy.start()
        clear_tail(keys, values)
        for copy in copies:
            copy.wait()

    fill_stack(qstack, q_ref)
    m_scr[...] = jnp.full_like(m_scr, -3e38)
    l_scr[...] = jnp.zeros_like(l_scr)
    ctx_t[...] = jnp.zeros_like(ctx_t)
    tab = tab_ref[...]

    def pass1(c, carry):
        base, doc = tile_of(tiles, qb, c)
        put_buckets(b_scr, kmeta_ref[pl.ds(base, KB), :], qmeta_ref[...], doc)

        def rows(g, carry):
            j = g * RB
            out = nn(tab, one_hot(b_scr, j, RB))
            for r in range(RB):
                bias_scr[pl.ds(j + r, 16, stride=KB), :] = out[:, r * QB : (r + 1) * QB]
            return carry

        lax.fori_loop(0, KB // RB, rows, 0, unroll=KB // RB)
        for p in range(PAIRS):
            raw = nt(keys[pl.ds(base, KB), 128 * p : 128 * p + 128], qstack[p])
            o = 8 + p
            s = raw + jnp.concatenate([bias_scr[p * KB : (p + 1) * KB, :], bias_scr[o * KB : (o + 1) * KB, :]], axis=1)
            s_scr[c, p] = s
            m_scr[p] = jnp.maximum(m_scr[p], jnp.max(s.reshape(KB // 8, 8, 2 * QB), axis=0))
        return carry

    lax.fori_loop(0, count, pass1, 0)
    for p in range(PAIRS):
        m_scr[p] = jnp.broadcast_to(jnp.max(m_scr[p], axis=0, keepdims=True), (8, 2 * QB))

    def pcopy(slot, c):
        return pltpu.make_async_copy(pbuf.at[slot], p_hbm.at[qb, c], sems.at[slot])

    def pass2(c, carry):
        base, _ = tile_of(tiles, qb, c)
        slot = lax.rem(c, 2)

        @pl.when(c >= 2)
        def _():
            pcopy(slot, c).wait()

        for p in range(PAIRS):
            e = jnp.exp(s_scr[c, p] - m_scr[p, 0:1, :])
            l_scr[p] = l_scr[p] + jnp.sum(e.reshape(KB // 8, 8, 2 * QB), axis=0)
            pb = e.astype(BF16)
            pbuf[slot, p] = pb
            value_t = values[pl.ds(base, KB), 128 * p : 128 * p + 128].T
            for h in range(2):
                r = 128 * p + 64 * h
                ctx_t[r : r + 64, :] = ctx_t[r : r + 64, :] + nn(value_t[64 * h : 64 * h + 64], pb[:, h * QB : (h + 1) * QB])
        pcopy(slot, c).start()
        return carry

    lax.fori_loop(0, count, pass2, 0)
    for p in range(PAIRS):
        inv = 1.0 / jnp.sum(l_scr[p], axis=0, keepdims=True)
        wide = jnp.concatenate([jnp.broadcast_to(inv[:, :QB], (64, QB)), jnp.broadcast_to(inv[:, QB:], (64, QB))], axis=0)
        w = slice(128 * p, 128 * p + 128)
        ctx_ref[:, w] = (ctx_t[w, :] * wide).T
        inv_ref[:, w] = wide.T

    @pl.when(count >= 2)
    def _():
        pcopy(lax.rem(count, 2), 0).wait()

    pcopy(lax.rem(count + 1, 2), 0).wait()


def attention_fwd(tiles, q, k, v, kmeta, qmeta, tab):
    rows, width = q.shape
    span = kmeta.shape[0]
    nq, nc = rows // QB, TILES
    vm = pltpu.VMEM
    hbm = pl.BlockSpec(memory_space=pl.ANY)
    full = lambda *s: pl.BlockSpec(s, lambda i, r: (0,) * len(s))
    block = pl.BlockSpec((QB, width), lambda i, r: (i, 0))
    return pl.pallas_call(
        fwd_kernel,
        grid_spec=pltpu.PrefetchScalarGridSpec(
            num_scalar_prefetch=1, grid=(nq,),
            in_specs=[block] + [hbm] * 2 + [full(span, 128), pl.BlockSpec((8, QB), lambda i, r: (0, i)), full(16, 160)],
            out_specs=[block, block, hbm],
            scratch_shapes=[
                vm((span, width), BF16), vm((span, width), BF16),
                vm((nc, PAIRS, KB, 2 * QB), F32), vm((3, KB, QB), F32), vm((16 * KB, QB), F32),
                vm((PAIRS, 2 * QB, 128), BF16), vm((width, QB), F32), vm((PAIRS, 8, 2 * QB), F32),
                vm((PAIRS, 8, 2 * QB), F32), vm((2, PAIRS, KB, 2 * QB), BF16),
                pltpu.SemaphoreType.DMA((2,)), pltpu.SemaphoreType.DMA((6,))]),
        out_shape=[jax.ShapeDtypeStruct((rows, width), F32), jax.ShapeDtypeStruct((rows, width), F32),
                   jax.ShapeDtypeStruct((nq, nc, PAIRS, KB, 2 * QB), BF16)],
        compiler_params=pltpu.CompilerParams(vmem_limit_bytes=56 * 2**20, dimension_semantics=("arbitrary",)),
        cost_estimate=pl.CostEstimate(flops=25 * 10**9, bytes_accessed=30 * 2**20, transcendentals=5 * 10**6),
        name="attention_forward",
    )(tiles, q, k, v, kmeta, qmeta, tab)


def order_tables(ts, tx, ty):
    t = jnp.concatenate([ts.at[16].set(NEG), tx, ty], axis=0).T
    z = jnp.zeros((2, 160), t.dtype)
    return jnp.concatenate([t[0::2], z, t[1::2], z], axis=0)


def bwd_kernel(tiles, q_ref, dc_ref, ctx_ref, k_hbm, v_hbm, kmeta_ref, qmeta_ref, p_hbm,
               dq_ref, dk_hbm, dv_hbm, dtab_ref,
               keys, values, dk, dv, dq_t, b_scr, ds_scr, delta, qstack, cstack, pbuf, sems, in_sems):
    qb = pl.program_id(0)
    last = pl.num_programs(0) - 1
    count = tiles[qb, 0]

    def pcopy(c):
        slot = lax.rem(c, 2)
        return pltpu.make_async_copy(p_hbm.at[qb, c], pbuf.at[slot], sems.at[slot])

    pcopy(0).start()

    @pl.when(qb == 0)
    def _():
        copies = window_copies(k_hbm, v_hbm, keys, values, in_sems)
        for copy in copies:
            copy.start()
        clear_tail(keys, values)
        dk[...] = jnp.zeros_like(dk)
        dv[...] = jnp.zeros_like(dv)
        dtab_ref[...] = jnp.zeros_like(dtab_ref)
        ds_scr[...] = jnp.zeros_like(ds_scr)
        for copy in copies:
            copy.wait()

    fill_stack(qstack, q_ref)
    fill_stack(cstack, dc_ref)
    for p in range(PAIRS):
        w = slice(128 * p, 128 * p + 128)
        both = (dc_ref[:, w].astype(F32) * ctx_ref[:, w]).T
        delta[p : p + 1, :] = jnp.concatenate(
            [jnp.sum(both[:64], axis=0, keepdims=True), jnp.sum(both[64:], axis=0, keepdims=True)], axis=1)
    dq_t[...] = jnp.zeros_like(dq_t)

    def tile(c, carry):
        base, doc = tile_of(tiles, qb, c)
        slot = lax.rem(c, 2)
        put_buckets(b_scr, kmeta_ref[pl.ds(base, KB), :], qmeta_ref[...], doc)

        @pl.when(c + 1 < count)
        def _():
            pcopy(c + 1).start()

        pcopy(c).wait()
        for p in range(PAIRS):
            w = slice(128 * p, 128 * p + 128)
            dp = nt(values[pl.ds(base, KB), w], cstack[p])
            pb = pbuf[slot, p]
            ds = pb.astype(F32) * (dp - delta[p : p + 1, :])
            ds_scr[p * KB : (p + 1) * KB, :] = ds[:, :QB]
            ds_scr[(8 + p) * KB : (9 + p) * KB, :] = ds[:, QB:]
            dsb = ds.astype(BF16)
            dk[pl.ds(base, KB), w] = dk[pl.ds(base, KB), w] + nn(dsb, qstack[p])
            dv[pl.ds(base, KB), w] = dv[pl.ds(base, KB), w] + nn(pb, cstack[p])
            key_t = keys[pl.ds(base, KB), w].T
            for h in range(2):
                r = 128 * p + 64 * h
                dq_t[r : r + 64, :] = dq_t[r : r + 64, :] + nn(key_t[64 * h : 64 * h + 64], dsb[:, h * QB : (h + 1) * QB])

        def rows(g, acc):
            j = g * RB
            d = jnp.concatenate([ds_scr[pl.ds(j + r, 16, stride=KB), :] for r in range(RB)], axis=1).astype(BF16)
            return acc + nt(d, one_hot(b_scr, j, RB))

        dtab_ref[...] = lax.fori_loop(0, KB // RB, rows, dtab_ref[...], unroll=KB // RB)
        return carry

    lax.fori_loop(0, count, tile, 0)
    for p in range(PAIRS):
        w = slice(128 * p, 128 * p + 128)
        dq_ref[:, w] = dq_t[w, :].T.astype(BF16)

    @pl.when(qb == last)
    def _():
        part = dk_hbm.shape[0] // 3
        copies = []
        for i in range(6):
            src, dst, out = ((dk, keys, dk_hbm), (dv, values, dv_hbm))[i % 2]
            start = i // 2 * part

            def move(j, carry):
                r = pl.multiple_of(start + j * 32, 32)
                dst[pl.ds(r, 32), :] = src[pl.ds(r, 32), :].astype(BF16)
                return carry

            lax.fori_loop(0, part // 32, move, 0)
            copy = pltpu.make_async_copy(dst.at[pl.ds(start, part), :], out.at[pl.ds(start, part), :], in_sems.at[i])
            copy.start()
            copies.append(copy)
        for copy in copies:
            copy.wait()


def attention_bwd(tiles, q, dc, ctx, k, v, kmeta, qmeta, probs):
    rows, width = q.shape
    span = kmeta.shape[0]
    nq, nc = rows // QB, TILES
    vm = pltpu.VMEM
    hbm = pl.BlockSpec(memory_space=pl.ANY)
    full = lambda *s: pl.BlockSpec(s, lambda i, r: (0,) * len(s))
    block = pl.BlockSpec((QB, width), lambda i, r: (i, 0))
    shape = jax.ShapeDtypeStruct
    return pl.pallas_call(
        bwd_kernel,
        grid_spec=pltpu.PrefetchScalarGridSpec(
            num_scalar_prefetch=1, grid=(nq,),
            in_specs=[block] * 3 + [hbm] * 2 + [full(span, 128), pl.BlockSpec((8, QB), lambda i, r: (0, i)), hbm],
            out_specs=[block, hbm, hbm, full(16, 160)],
            scratch_shapes=[
                vm((span, width), BF16), vm((span, width), BF16),
                vm((span, width), F32), vm((span, width), F32), vm((width, QB), F32),
                vm((3, KB, QB), F32), vm((16 * KB, QB), F32), vm((8, 2 * QB), F32),
                vm((PAIRS, 2 * QB, 128), BF16), vm((PAIRS, 2 * QB, 128), BF16),
                vm((2, PAIRS, KB, 2 * QB), BF16), pltpu.SemaphoreType.DMA((2,)), pltpu.SemaphoreType.DMA((6,))]),
        out_shape=[shape((rows, width), BF16), shape(k.shape, BF16), shape(k.shape, BF16), shape((16, 160), F32)],
        compiler_params=pltpu.CompilerParams(vmem_limit_bytes=56 * 2**20, dimension_semantics=("arbitrary",)),
        cost_estimate=pl.CostEstimate(flops=40 * 10**9, bytes_accessed=40 * 2**20, transcendentals=0),
        name="attention_backward",
    )(tiles, q, dc, ctx, k, v, kmeta, qmeta, probs)


def exchange_plan(n_seq, n_ffn, half):
    seq_bits = [("seq", 1 << b) for b in range(n_seq.bit_length() - 1)]
    ffn_bits = [("ffn", 1 << b) for b in range(1, n_ffn.bit_length() - 1)]
    unit = 16 * n_seq * n_ffn // 2
    if half % (3 * unit) == 0:
        orders = [seq_bits + ffn_bits, ffn_bits + seq_bits, ffn_bits[1:] + seq_bits + ffn_bits[:1]]
        return orders, half // 3
    return [seq_bits + ffn_bits], half


def sum_kernel(orders, length, a_ref, small_ref, out_ref, small_out, work, core_in, slots, sums, small_in,
               core_sems, core_back, send_sems, recv_sems, back_send, back_recv, small_send, small_recv):
    seq, ffn = lax.axis_index("seq"), lax.axis_index("ffn")
    half = work.shape[0]
    streams = len(orders)
    steps = len(orders[0])
    core = lax.rem(ffn, 2)

    def bit_of(axis, bit):
        return lax.rem((seq if axis == "seq" else ffn) // bit, 2)

    def partner(axis, bit):
        flip = bit * (1 - 2 * bit_of(axis, bit))
        return {axis: (seq if axis == "seq" else ffn) + flip}

    peers = [("ffn", 1)] + sorted(orders[0])
    barrier = pltpu.get_barrier_semaphore()
    for axis, bit in peers:
        pl.semaphore_signal(barrier, inc=1, device_id=partner(axis, bit), device_id_type=pl.DeviceIdType.MESH)
    pl.semaphore_wait(barrier, len(peers))

    def remote(src, dst, send, recv, axis, bit):
        return pltpu.make_async_remote_copy(src_ref=src, dst_ref=dst, send_sem=send, recv_sem=recv,
                                            device_id=partner(axis, bit), device_id_type=pl.DeviceIdType.MESH)

    def at(ref, start, size):
        return ref.at[pl.ds(start if isinstance(start, int) else pl.multiple_of(start, 16), size), :]

    def add(dst, dst_lo, one, one_lo, two, two_lo, size):
        def body(i, carry):
            r = i * 16
            dst[pl.ds(pl.multiple_of(dst_lo + r, 16), 16), :] = (
                one[pl.ds(pl.multiple_of(one_lo + r, 16), 16), :].astype(F32)
                + two[pl.ds(pl.multiple_of(two_lo + r, 16), 16), :].astype(F32)
            ).astype(BF16)
            return carry
        lax.fori_loop(0, size // 16, body, 0)

    pending = []
    firsts = []
    for s in range(streams):
        copy = remote(at(a_ref, (1 - core) * half + s * length, length), at(core_in, s * length, length),
                      core_sems.at[s], core_sems.at[streams + s], "ffn", 1)
        copy.start()
        firsts.append(copy)
    sums[0] = small_ref[...]

    def small_copy(k):
        axis, bit = peers[k]
        return remote(sums.at[k], small_in.at[k], small_send.at[k], small_recv.at[k], axis, bit)
    small_copy(0).start()

    lows = [s * length for s in range(streams)]
    sizes = [length] * streams
    offs = []
    base = 0
    for s in range(streams):
        own = []
        size = length
        for k in range(steps):
            size //= 2
            own.append((base, size))
            base += size
        offs.append(own)

    def scatter(s, k):
        axis, bit = orders[s][k]
        size = sizes[s] // 2
        mine = lows[s] + bit_of(axis, bit) * size
        theirs = lows[s] + (1 - bit_of(axis, bit)) * size
        slot, _ = offs[s][k]
        copy = remote(at(work, theirs, size), at(slots, slot, size), send_sems.at[s, k], recv_sems.at[s, k], axis, bit)
        copy.start()
        return copy, mine, size

    flying = []
    for s in range(streams):
        firsts[s].wait_recv()
        add(work, s * length, a_ref, core * half + s * length, core_in, s * length, length)
        flying.append(scatter(s, 0))
    for k in range(steps):
        for s in range(streams):
            copy, mine, size = flying[s]
            copy.wait_recv()
            slot, _ = offs[s][k]
            last = k == steps - 1
            if last:
                add(out_ref, core * half + mine, work, mine, slots, slot, size)
            else:
                add(work, mine, work, mine, slots, slot, size)
            pending.append(copy)
            lows[s], sizes[s] = mine, size
            if not last:
                flying[s] = scatter(s, k + 1)
            else:
                flying[s] = gather(s, k, lows, sizes, orders, remote, at, out_ref, core, half, back_send, back_recv)
        small_copy(k).wait_recv()
        sums[k + 1] = sums[k] + small_in[k]
        small_copy(k + 1).start()
    small_copy(steps).wait_recv()
    small_out[...] = sums[steps] + small_in[steps]
    finals = []
    for k in range(steps - 1, -1, -1):
        for s in range(streams):
            copy = flying[s]
            copy.wait_recv()
            pending.append(copy)
            axis, bit = orders[s][k]
            lows[s] = lows[s] - bit_of(axis, bit) * sizes[s]
            sizes[s] = 2 * sizes[s]
            if k:
                flying[s] = gather(s, k - 1, lows, sizes, orders, remote, at, out_ref, core, half, back_send, back_recv)
            else:
                copy = remote(at(out_ref, core * half + s * length, length), at(out_ref, core * half + s * length, length),
                              core_back.at[s], core_back.at[streams + s], "ffn", 1)
                copy.start()
                finals.append(copy)
    for copy in finals:
        copy.wait_recv()
    for copy in firsts + pending + finals:
        copy.wait_send()
    for k in range(steps + 1):
        small_copy(k).wait_send()


def gather(s, k, lows, sizes, orders, remote, at, out_ref, core, half, back_send, back_recv):
    axis, bit = orders[s][k]
    place = at(out_ref, core * half + lows[s], sizes[s])
    copy = remote(place, place, back_send.at[s, k], back_recv.at[s, k], axis, bit)
    copy.start()
    return copy


def sum_everywhere(a, small):
    n_seq, n_ffn = lax.axis_size("seq"), lax.axis_size("ffn")
    grain = 16 * n_seq * n_ffn // 2
    rows, width = a.shape
    half = -(-(rows // 2) // grain) * grain
    if 2 * half > rows:
        a = jnp.pad(a, ((0, 2 * half - rows), (0, 0)))
    orders, length = exchange_plan(n_seq, n_ffn, half)
    streams, steps = len(orders), len(orders[0])
    vm, dma = pltpu.VMEM, pltpu.SemaphoreType.DMA
    slot_rows = streams * (length - length // (1 << steps))
    out, small_out = pl.pallas_call(
        functools.partial(sum_kernel, orders, length),
        out_shape=[jax.ShapeDtypeStruct(a.shape, BF16), jax.ShapeDtypeStruct(small.shape, F32)],
        in_specs=[pl.BlockSpec(memory_space=vm)] * 2,
        out_specs=[pl.BlockSpec(memory_space=vm)] * 2,
        scratch_shapes=[
            vm((half, width), BF16), vm((half, width), BF16), vm((slot_rows, width), BF16),
            vm((steps + 1,) + small.shape, F32), vm((steps + 1,) + small.shape, F32),
            dma((2 * streams,)), dma((2 * streams,)), dma((streams, steps)), dma((streams, steps)),
            dma((streams, steps)), dma((streams, steps)), dma((steps + 1,)), dma((steps + 1,)),
        ],
        compiler_params=pltpu.CompilerParams(collective_id=0, has_side_effects=True, vmem_limit_bytes=48 * 2**20),
        name="sum_everywhere",
    )(a, small)
    return out[:rows], small_out


UB = 512


def gelu_and_slope(x):
    z = jnp.abs(x) * 0.7071067811865476
    t = 1.0 / (1.0 + 0.3275911 * z)
    poly = ((((1.061405429 * t - 1.453152027) * t + 1.421413741) * t - 0.284496736) * t + 0.254829592) * t
    bell = jnp.exp(-z * z)
    tail = 0.5 * poly * bell
    phi = jnp.where(x < 0, tail, 1.0 - tail)
    return x * phi, phi + x * bell * 0.3989422804014327


def tn(a, b):
    return lax.dot_general(a, b, (((0,), (0,)), ((), ())), preferred_element_type=F32)


def ffn_up_kernel(normed_ref, up_ref, active_ref, slope_ref):
    rows = normed_ref.shape[0]
    size = rows // 2
    for r in range(0, rows, size):
        w = slice(r, r + size)
        act, slope = gelu_and_slope(nt(normed_ref[w, :], up_ref[...]))
        active_ref[w, :] = act.astype(BF16)
        slope_ref[w, :] = slope.astype(BF16)


def ffn_up(normed, up):
    rows, wide = normed.shape
    units = up.shape[0]
    full = lambda *s: pl.BlockSpec(s, lambda i: (0,) * len(s))
    col = pl.BlockSpec((rows, UB), lambda i: (0, i))
    shape = jax.ShapeDtypeStruct
    return pl.pallas_call(
        ffn_up_kernel,
        grid=(units // UB,),
        in_specs=[full(rows, wide), pl.BlockSpec((UB, wide), lambda i: (i, 0))],
        out_specs=[col, col],
        out_shape=[shape((rows, units), BF16), shape((rows, units), BF16)],
        compiler_params=pltpu.CompilerParams(vmem_limit_bytes=48 * 2**20, dimension_semantics=("arbitrary",)),
        cost_estimate=pl.CostEstimate(flops=2 * rows * units * wide, bytes_accessed=15 * 2**20, transcendentals=2 * rows * units),
        name="ffn_up",
    )(normed, up)


def ffn_back_kernel(grad_ref, normed_ref, up_ref, down_ref, active_ref, slope_ref, unit_ref, bias_ref, normed_grad_ref):
    @pl.when(pl.program_id(0) == 0)
    def _():
        normed_grad_ref[...] = jnp.zeros_like(normed_grad_ref)

    grad = grad_ref[...]
    width = grad.shape[1]
    unit_ref[:, width:] = tn(active_ref[...], grad).astype(BF16)
    pre = (nt(grad, down_ref[...]) * slope_ref[...].astype(F32)).astype(BF16)
    up_grad = tn(pre, normed_ref[...])
    unit_ref[:, :width] = up_grad[:, :width].astype(BF16)
    bias_ref[...] = up_grad[:, width:]
    normed_grad_ref[...] = normed_grad_ref[...] + nn(pre, up_ref[:, :width])


def ffn_back(grad, normed, up, down, active, slope):
    rows, wide = normed.shape
    units, width = down.shape
    full = lambda *s: pl.BlockSpec(s, lambda i: (0,) * len(s))
    col = pl.BlockSpec((rows, UB), lambda i: (0, i))
    row = lambda n: pl.BlockSpec((UB, n), lambda i: (i, 0))
    shape = jax.ShapeDtypeStruct
    return pl.pallas_call(
        ffn_back_kernel,
        grid=(units // UB,),
        in_specs=[full(rows, width), full(rows, wide), row(wide), row(width), col, col],
        out_specs=[row(2 * width), row(wide - width), full(rows, width)],
        out_shape=[shape((units, 2 * width), BF16), shape((units, wide - width), F32), shape((rows, width), F32)],
        compiler_params=pltpu.CompilerParams(vmem_limit_bytes=48 * 2**20, dimension_semantics=("arbitrary",)),
        cost_estimate=pl.CostEstimate(flops=4 * rows * units * (wide + width), bytes_accessed=30 * 2**20, transcendentals=0),
        name="ffn_back",
    )(grad, normed, up, down, active, slope)


def from_behind(x, axis, by):
    devices = lax.axis_size(axis)
    pairs = [(i, i + by) for i in range(devices) if 0 <= i + by < devices]
    return lax.ppermute(x, axis, pairs)


def layer_norm(value, gain, shift):
    center = value - jnp.mean(value, axis=-1, keepdims=True)
    spread = jnp.mean(center * center, axis=-1, keepdims=True)
    return center * lax.rsqrt(spread + norm_eps) * gain + shift


def layout(row_ids, doc_ends):
    forwarded_value = row_ids[:, None] >= doc_ends[None, :]
    doc_ids = jnp.sum(forwarded_value.astype(jnp.int32), axis=1)
    starts = jnp.max(jnp.where(forwarded_value, doc_ends[None, :], 0), axis=1)
    offsets = row_ids - starts
    places = jnp.where(offsets < VISUAL, offsets, offsets - VISUAL)
    return (doc_ids, places)


def tile_table(starts, doc_ids, key_docs, window_start, rows):
    docs = jnp.arange(starts.shape[0] - 1, dtype=jnp.int32)
    place = jnp.arange(doc_ids.shape[0], dtype=jnp.int32)
    ends = jnp.max(jnp.where(key_docs[None, :] == docs[:, None], place[None, :] + 1, 0), axis=1)
    own = doc_ids[rows : 2 * rows]
    segments = own[0::QB, None] + jnp.arange(3, dtype=jnp.int32)[None, :]
    active = segments <= own[QB - 1 :: QB, None]
    hit = segments[:, :, None] == docs[None, None, :]
    low = jnp.sum(jnp.where(hit, starts[None, None, :-1], 0), axis=2) - window_start
    low = jnp.maximum(low, 0) // 16 * 16
    high = jnp.sum(jnp.where(hit, ends[None, None, :], 0), axis=2)
    count = jnp.where(active, jnp.maximum(high - low + KB - 1, 0) // KB, 0)
    before = jnp.cumsum(count, axis=1) - count
    index = jnp.arange(TILES, dtype=jnp.int32)[None, None, :] - before[:, :, None]
    inside = (index >= 0) & (index < count[:, :, None])
    base = jnp.sum(jnp.where(inside, low[:, :, None] + KB * index, 0), axis=1)
    doc = jnp.sum(jnp.where(inside, segments[:, :, None], 0), axis=1)
    return jnp.concatenate([jnp.sum(count, axis=1, keepdims=True), base, doc], axis=1).astype(jnp.int32)


def on_device(
    hidden_in, doc_lengths, box_x, box_y, token_valid, w_query, b_query, w_key, w_value, b_value,
    w_out, b_out, gain_attn, shift_attn, w_up, b_up, w_down, b_down, gain_out, shift_out,
    table_seq, table_x, table_y, out_grad,
):
    rows = hidden_in.shape[0]
    width = hidden_in.shape[1]
    heads = table_seq.shape[1]
    group_rows = box_x.shape[0]
    span = 3 * rows
    first_row = lax.axis_index("ffn") * rows
    doc_ends = jnp.cumsum(doc_lengths[0])

    n_ffn = lax.axis_size("ffn")
    n_seq = lax.axis_size("seq")
    up = [(i, i + 1) for i in range(n_ffn - 1)]
    hidden_low = lax.ppermute(hidden_in, "ffn", up)
    hidden_high = lax.ppermute(hidden_in, "ffn", [(j, i) for i, j in up])

    units = b_up.shape[0]
    up_ext = jnp.concatenate([w_up.T, b_up[:, None], jnp.zeros((units, 127), BF16)], axis=1)
    later, up_ext = lax.optimization_barrier((w_down, up_ext))
    up_all = lax.all_gather(up_ext, "ffn", axis=0, tiled=True)
    down_all = lax.all_gather(later, "ffn", axis=0, tiled=True)

    window_rows = first_row - rows + jnp.arange(span, dtype=jnp.int32)
    doc_ids, places = layout(window_rows, doc_ends)
    inside = (window_rows >= 0) & (window_rows < group_rows)

    def window_of(item):
        edge = jnp.zeros((rows,), item.dtype)
        padded = jnp.concatenate([edge, item, edge])
        return lax.dynamic_slice_in_dim(padded, first_row, span)

    win_x, win_y = window_of(box_x), window_of(box_y)
    key_open = (window_of(token_valid) == 1) & inside
    key_docs = jnp.where(key_open, doc_ids, -1)
    kmeta = jnp.stack([places, win_x, win_y, key_docs], axis=1).astype(F32)
    kmeta = jnp.pad(kmeta, ((0, KB), (0, 124)), constant_values=-1.0)
    own = slice(rows, 2 * rows)
    qmeta = jnp.stack([places[own], win_x[own], win_y[own], doc_ids[own]], axis=0).astype(F32)
    qmeta = jnp.pad(qmeta, ((0, 4), (0, 0)))
    starts = jnp.concatenate([jnp.zeros((1,), doc_ends.dtype), doc_ends])
    tiles = tile_table(starts, doc_ids, key_docs, first_row - rows, rows)
    tables = order_tables(table_seq, table_x, table_y)

    query = ((jnp.dot(hidden_in, w_query, preferred_element_type=F32) + b_query) * 0.125).astype(BF16)
    window = jnp.concatenate([hidden_low, hidden_in, hidden_high], axis=0)
    key = jnp.dot(window, w_key, preferred_element_type=F32).astype(BF16)
    value = (jnp.dot(window, w_value, preferred_element_type=F32) + b_value).astype(BF16)

    context, inv, probs = attention_fwd(tiles, query, key, value, kmeta, qmeta, tables)
    context_low = context.astype(BF16)
    attn = jnp.dot(context_low, w_out, preferred_element_type=F32) + b_out
    inputs = hidden_in.astype(F32)
    normed, norm_pull = jax.vjp(
        layer_norm, inputs + attn, gain_attn.astype(F32), shift_attn.astype(F32)
    )
    normed_low = normed.astype(BF16)
    ones = jnp.concatenate([jnp.ones((rows, 1), BF16), jnp.zeros((rows, 127), BF16)], axis=1)
    normed_ext = jnp.concatenate([normed_low, ones], axis=1)
    active, slope = ffn_up(normed_ext, up_all)
    branch = jnp.dot(active, down_all, preferred_element_type=F32)
    hidden_out, out_pull = jax.vjp(
        layer_norm, normed + (branch + b_down), gain_out.astype(F32), shift_out.astype(F32)
    )
    mid_grad, grad_gain_out, grad_shift_out = out_pull(out_grad.astype(F32))
    branch_grad = mid_grad.astype(BF16)
    grad_b_down = jnp.sum(branch_grad.astype(F32), axis=0)
    unit_part, bias_part, branch_back = ffn_back(branch_grad, normed_ext, up_all, down_all, active, slope)
    unit_grad = lax.psum_scatter(unit_part, "ffn", scatter_dimension=0, tiled=True)
    normed_grad = mid_grad + branch_back
    mid1_grad, grad_gain_attn, grad_shift_attn = norm_pull(normed_grad)
    attn_grad = mid1_grad.astype(BF16)
    grad_b_out = jnp.sum(attn_grad.astype(F32), axis=0)
    grad_w_out = jnp.dot(context_low.T, attn_grad, preferred_element_type=F32)
    scaled = (nt(attn_grad, w_out) * inv).astype(BF16)
    query_grad, key_grad, value_grad, table_sum = attention_bwd(
        tiles, query, scaled, context, key, value, kmeta, qmeta, probs
    )
    def through(part):
        return nt(key_grad[part], w_key) + nt(value_grad[part], w_value)

    from_below = from_behind(through(slice(2 * rows, span)).astype(BF16), "ffn", 1)
    from_above = from_behind(through(slice(0, rows)).astype(BF16), "ffn", -1)
    big = jnp.concatenate(
        [
            (jnp.dot(hidden_in.T, query_grad, preferred_element_type=F32) * 0.125).astype(BF16),
            jnp.dot(window.T, key_grad, preferred_element_type=F32).astype(BF16),
            jnp.dot(window.T, value_grad, preferred_element_type=F32).astype(BF16),
            grad_w_out.astype(BF16),
        ],
        axis=0,
    )
    small = jnp.stack(
        [
            jnp.sum(query_grad.astype(F32), axis=0) * 0.125,
            jnp.sum(value_grad.astype(F32), axis=0),
            grad_b_out,
            grad_gain_attn,
            grad_shift_attn,
            grad_b_down,
            grad_gain_out,
            grad_shift_out,
        ]
    )
    levels = table_sum.shape[1]
    small = jnp.concatenate(
        [small, jnp.pad(table_sum, ((0, 0), (0, width - levels))), bias_part[:, 0].reshape(-1, width)], axis=0
    )
    big, small = sum_everywhere(big, small)
    big, small, unit_grad, query_grad, key_grad, value_grad, from_below, from_above = lax.optimization_barrier(
        (big, small, unit_grad, query_grad, key_grad, value_grad, from_below, from_above)
    )
    for b in range(n_seq.bit_length() - 1):
        unit_grad = unit_grad + lax.ppermute(unit_grad, "seq", [(i, i ^ (1 << b)) for i in range(n_seq)])
    unit_grad = unit_grad.astype(F32)
    hidden_grad = (
        mid1_grad + nt(query_grad, w_query) * 0.125 + through(own) + from_below.astype(F32) + from_above.astype(F32)
    )
    grad_w_up = unit_grad[:, :width].T
    grad_w_down = unit_grad[:, width:]
    grad_b_up = lax.dynamic_slice_in_dim(small[24:].reshape(-1), lax.axis_index("ffn") * units, units)
    grads = [big[i * width : (i + 1) * width].astype(F32) for i in range(4)]
    vec = [small[i] for i in range(8)]
    table_all = jnp.stack([small[8 + h // 2 + 8 * (h % 2), :levels] for h in range(heads)], axis=1)
    return (
        hidden_out, hidden_grad, grads[0], vec[0], grads[1], grads[2], vec[1], grads[3], vec[2], vec[3], vec[4],
        grad_w_up, grad_b_up, grad_w_down, vec[5], vec[6], vec[7],
        table_all[:32], table_all[32:96], table_all[96:],
    )


def solution(mesh):
    in_specs = (
        P(("seq", "ffn"), None),
        P("seq", None),
        P("seq"),
        P("seq"),
        P("seq"),
        P(),
        P(),
        P(),
        P(),
        P(),
        P(),
        P(),
        P(),
        P(),
        P(None, "ffn"),
        P("ffn"),
        P("ffn", None),
        P(),
        P(),
        P(),
        P(),
        P(),
        P(),
        P(("seq", "ffn"), None),
    )
    out_specs = (
        P(("seq", "ffn"), None),
        P(("seq", "ffn"), None),
        P(),
        P(),
        P(),
        P(),
        P(),
        P(),
        P(),
        P(),
        P(),
        P(None, "ffn"),
        P("ffn"),
        P("ffn", None),
        P(),
        P(),
        P(),
        P(),
        P(),
        P(),
    )
    return jax.shard_map(
        on_device, mesh=mesh, in_specs=in_specs, out_specs=out_specs, check_vma=False
    )
```

```python
import functools

import jax
import jax.numpy as jnp
from jax import lax
from jax.experimental import pallas as pl
from jax.experimental.pallas import tpu as pltpu
from jax.sharding import PartitionSpec as P

VISUAL = 49
norm_eps = 1e-12
F32 = jnp.float32
BF16 = jnp.bfloat16
QB = 128
KB = 128
RB = 16
PAIRS = 6
NEG = -1e30
TILES = 12


def nn(a, b):
    return lax.dot_general(a, b, (((1,), (0,)), ((), ())), preferred_element_type=F32)


def nt(a, b):
    return lax.dot_general(a, b, (((1,), (1,)), ((), ())), preferred_element_type=F32)


def log_bucket(d, near, per_octave, sign):
    mag = jnp.abs(d)
    far = jnp.floor(jnp.log2(jnp.maximum(mag, 1.0) * (1.0 / near)) * per_octave + 0.0002) + near
    far = jnp.minimum(far, 2.0 * near - 1.0)
    return jnp.where(mag < near, mag, far) + jnp.where(d > 0, F32(sign), F32(0))


def put_buckets(b_ref, kmeta, qmeta, doc):
    key_doc = jnp.where(kmeta[:, 3:4] == doc.astype(F32), kmeta[:, 3:4], -1.0)
    same = key_doc == qmeta[3:4, :]
    b_ref[0] = jnp.where(same, log_bucket(kmeta[:, 0:1] - qmeta[0:1, :], 8.0, 2.0, 16.0), 16.0)
    b_ref[1] = log_bucket(kmeta[:, 1:2] - qmeta[1:2, :], 16.0, 4.0, 32.0)
    b_ref[2] = log_bucket(kmeta[:, 2:3] - qmeta[2:3, :], 16.0, 4.0, 32.0)


def one_hot(b_ref, row, count):
    cols = []
    for r in range(count):
        parts = []
        for t, size in ((0, 32), (1, 64), (2, 64)):
            v = jnp.broadcast_to(b_ref[t, pl.ds(row + r, 1), :], (size, QB)).astype(BF16)
            levels = lax.broadcasted_iota(jnp.int32, (size, QB), 0).astype(F32).astype(BF16)
            parts.append(jnp.where(v == levels, BF16(1), BF16(0)))
        cols.append(jnp.concatenate(parts, axis=0))
    return jnp.concatenate(cols, axis=1)


def fill_stack(stack, src):
    lane = lax.broadcasted_iota(jnp.int32, (QB, 128), 1)
    for p in range(PAIRS):
        x = src[:, 128 * p : 128 * p + 128].astype(F32)
        stack[p, 0:QB, :] = jnp.where(lane < 64, x, 0.0).astype(BF16)
        stack[p, QB : 2 * QB, :] = jnp.where(lane < 64, 0.0, x).astype(BF16)


PARTS = 8


def window_copies(k_hbm, v_hbm, keys, values, sems):
    part = k_hbm.shape[0] // PARTS
    return [
        pltpu.make_async_copy(
            (k_hbm, v_hbm)[j].at[pl.ds(i * part, part), :], (keys, values)[j].at[pl.ds(i * part, part), :], sems.at[2 * i + j]
        )
        for i in range(PARTS)
        for j in range(2)
    ]


def clear_tail(keys, values):
    for ref in (keys, values):
        ref[ref.shape[0] - KB :, :] = jnp.zeros((KB, ref.shape[1]), ref.dtype)


def tile_of(tiles, qb, t):
    return pl.multiple_of(tiles[qb, 1 + t], 16), tiles[qb, 1 + TILES + t]


def fwd_kernel(tiles, q_ref, k_hbm, v_hbm, kmeta_ref, qmeta_ref, tab_ref, ctx_ref, inv_ref, p_hbm,
               keys, values, s_scr, b_scr, bias_scr, qstack, ctx_t, m_scr, l_scr, pbuf, sems, in_sems):
    qb = pl.program_id(0)
    count = tiles[qb, 0]

    @pl.when(qb == 0)
    def _():
        copies = window_copies(k_hbm, v_hbm, keys, values, in_sems)
        for copy in copies:
            copy.start()
        clear_tail(keys, values)
        for copy in copies:
            copy.wait()

    fill_stack(qstack, q_ref)
    m_scr[...] = jnp.full_like(m_scr, -3e38)
    l_scr[...] = jnp.zeros_like(l_scr)
    ctx_t[...] = jnp.zeros_like(ctx_t)
    tab = tab_ref[...]

    def pass1(c, carry):
        base, doc = tile_of(tiles, qb, c)
        put_buckets(b_scr, kmeta_ref[pl.ds(base, KB), :], qmeta_ref[...], doc)

        def rows(g, carry):
            j = g * RB
            out = nn(tab, one_hot(b_scr, j, RB))
            for r in range(RB):
                bias_scr[pl.ds(j + r, 16, stride=KB), :] = out[:, r * QB : (r + 1) * QB]
            return carry

        lax.fori_loop(0, KB // RB, rows, 0, unroll=KB // RB)
        for p in range(PAIRS):
            raw = nt(keys[pl.ds(base, KB), 128 * p : 128 * p + 128], qstack[p])
            o = 8 + p
            s = raw + jnp.concatenate([bias_scr[p * KB : (p + 1) * KB, :], bias_scr[o * KB : (o + 1) * KB, :]], axis=1)
            s_scr[c, p] = s
            m_scr[p] = jnp.maximum(m_scr[p], jnp.max(s.reshape(KB // 8, 8, 2 * QB), axis=0))
        return carry

    lax.fori_loop(0, count, pass1, 0)
    for p in range(PAIRS):
        m_scr[p] = jnp.broadcast_to(jnp.max(m_scr[p], axis=0, keepdims=True), (8, 2 * QB))

    def pcopy(slot, c):
        return pltpu.make_async_copy(pbuf.at[slot], p_hbm.at[qb, c], sems.at[slot])

    def pass2(c, carry):
        base, _ = tile_of(tiles, qb, c)
        slot = lax.rem(c, 2)

        @pl.when(c >= 2)
        def _():
            pcopy(slot, c).wait()

        for p in range(PAIRS):
            e = jnp.exp(s_scr[c, p] - m_scr[p, 0:1, :])
            l_scr[p] = l_scr[p] + jnp.sum(e.reshape(KB // 8, 8, 2 * QB), axis=0)
            pb = e.astype(BF16)
            pbuf[slot, p] = pb
            value_t = values[pl.ds(base, KB), 128 * p : 128 * p + 128].T
            for h in range(2):
                r = 128 * p + 64 * h
                ctx_t[r : r + 64, :] = ctx_t[r : r + 64, :] + nn(value_t[64 * h : 64 * h + 64], pb[:, h * QB : (h + 1) * QB])
        pcopy(slot, c).start()
        return carry

    lax.fori_loop(0, count, pass2, 0)
    for p in range(PAIRS):
        inv = 1.0 / jnp.sum(l_scr[p], axis=0, keepdims=True)
        wide = jnp.concatenate([jnp.broadcast_to(inv[:, :QB], (64, QB)), jnp.broadcast_to(inv[:, QB:], (64, QB))], axis=0)
        w = slice(128 * p, 128 * p + 128)
        ctx_ref[:, w] = (ctx_t[w, :] * wide).T
        inv_ref[:, w] = wide.T

    @pl.when(count >= 2)
    def _():
        pcopy(lax.rem(count, 2), 0).wait()

    pcopy(lax.rem(count + 1, 2), 0).wait()


def attention_fwd(tiles, q, k, v, kmeta, qmeta, tab):
    rows, width = q.shape
    span = kmeta.shape[0]
    nq, nc = rows // QB, TILES
    vm = pltpu.VMEM
    hbm = pl.BlockSpec(memory_space=pl.ANY)
    full = lambda *s: pl.BlockSpec(s, lambda i, r: (0,) * len(s))
    block = pl.BlockSpec((QB, width), lambda i, r: (i, 0))
    return pl.pallas_call(
        fwd_kernel,
        grid_spec=pltpu.PrefetchScalarGridSpec(
            num_scalar_prefetch=1, grid=(nq,),
            in_specs=[block] + [hbm] * 2 + [full(span, 128), pl.BlockSpec((8, QB), lambda i, r: (0, i)), full(16, 160)],
            out_specs=[block, block, hbm],
            scratch_shapes=[
                vm((span, width), BF16), vm((span, width), BF16),
                vm((nc, PAIRS, KB, 2 * QB), F32), vm((3, KB, QB), F32), vm((16 * KB, QB), F32),
                vm((PAIRS, 2 * QB, 128), BF16), vm((width, QB), F32), vm((PAIRS, 8, 2 * QB), F32),
                vm((PAIRS, 8, 2 * QB), F32), vm((2, PAIRS, KB, 2 * QB), BF16),
                pltpu.SemaphoreType.DMA((2,)), pltpu.SemaphoreType.DMA((2 * PARTS,))]),
        out_shape=[jax.ShapeDtypeStruct((rows, width), F32), jax.ShapeDtypeStruct((rows, width), F32),
                   jax.ShapeDtypeStruct((nq, nc, PAIRS, KB, 2 * QB), BF16)],
        compiler_params=pltpu.CompilerParams(vmem_limit_bytes=56 * 2**20, dimension_semantics=("arbitrary",)),
        cost_estimate=pl.CostEstimate(flops=25 * 10**9, bytes_accessed=30 * 2**20, transcendentals=5 * 10**6),
        name="attention_forward",
    )(tiles, q, k, v, kmeta, qmeta, tab)


def order_tables(ts, tx, ty):
    t = jnp.concatenate([ts.at[16].set(NEG), tx, ty], axis=0).T
    z = jnp.zeros((2, 160), t.dtype)
    return jnp.concatenate([t[0::2], z, t[1::2], z], axis=0)


def bwd_kernel(tiles, q_ref, dc_ref, ctx_ref, k_hbm, v_hbm, kmeta_ref, qmeta_ref, p_hbm,
               dq_ref, dk_hbm, dv_hbm, dtab_ref,
               keys, values, dk, dv, dq_t, b_scr, ds_scr, delta, qstack, cstack, pbuf, sems, in_sems):
    qb = pl.program_id(0)
    last = pl.num_programs(0) - 1
    count = tiles[qb, 0]

    before = jnp.int32(0)
    for b in range(dk.shape[0] // (3 * QB)):
        before = before + jnp.where(b < qb, tiles[b, 0], 0)

    def pcopy(block, c, slot):
        return pltpu.make_async_copy(p_hbm.at[block, c], pbuf.at[slot], sems.at[slot])

    @pl.when(qb == 0)
    def _():
        pcopy(0, 0, 0).start()
        copies = window_copies(k_hbm, v_hbm, keys, values, in_sems)
        for copy in copies:
            copy.start()
        clear_tail(keys, values)
        dk[...] = jnp.zeros_like(dk)
        dv[...] = jnp.zeros_like(dv)
        dtab_ref[...] = jnp.zeros_like(dtab_ref)
        ds_scr[...] = jnp.zeros_like(ds_scr)
        for copy in copies:
            copy.wait()

    fill_stack(qstack, q_ref)
    fill_stack(cstack, dc_ref)
    for p in range(PAIRS):
        w = slice(128 * p, 128 * p + 128)
        both = (dc_ref[:, w].astype(F32) * ctx_ref[:, w]).T
        delta[p : p + 1, :] = jnp.concatenate(
            [jnp.sum(both[:64], axis=0, keepdims=True), jnp.sum(both[64:], axis=0, keepdims=True)], axis=1)
    dq_t[...] = jnp.zeros_like(dq_t)

    def tile(c, carry):
        base, doc = tile_of(tiles, qb, c)
        slot = lax.rem(before + c, 2)

        @pl.when(c + 1 < count)
        def _():
            pcopy(qb, c + 1, 1 - slot).start()

        @pl.when((c + 1 == count) & (qb < last))
        def _():
            pcopy(qb + 1, 0, 1 - slot).start()

        put_buckets(b_scr, kmeta_ref[pl.ds(base, KB), :], qmeta_ref[...], doc)
        pcopy(qb, c, slot).wait()
        for p in range(PAIRS):
            w = slice(128 * p, 128 * p + 128)
            dp = nt(values[pl.ds(base, KB), w], cstack[p])
            pb = pbuf[slot, p]
            ds = pb.astype(F32) * (dp - delta[p : p + 1, :])
            ds_scr[p * KB : (p + 1) * KB, :] = ds[:, :QB]
            ds_scr[(8 + p) * KB : (9 + p) * KB, :] = ds[:, QB:]
            dsb = ds.astype(BF16)
            dk[pl.ds(base, KB), w] = dk[pl.ds(base, KB), w] + nn(dsb, qstack[p])
            dv[pl.ds(base, KB), w] = dv[pl.ds(base, KB), w] + nn(pb, cstack[p])
            key_t = keys[pl.ds(base, KB), w].T
            for h in range(2):
                r = 128 * p + 64 * h
                dq_t[r : r + 64, :] = dq_t[r : r + 64, :] + nn(key_t[64 * h : 64 * h + 64], dsb[:, h * QB : (h + 1) * QB])

        def rows(g, acc):
            j = g * RB
            d = jnp.concatenate([ds_scr[pl.ds(j + r, 16, stride=KB), :] for r in range(RB)], axis=1).astype(BF16)
            return acc + nt(d, one_hot(b_scr, j, RB))

        dtab_ref[...] = lax.fori_loop(0, KB // RB, rows, dtab_ref[...], unroll=KB // RB)
        return carry

    lax.fori_loop(0, count, tile, 0)
    for p in range(PAIRS):
        w = slice(128 * p, 128 * p + 128)
        dq_ref[:, w] = dq_t[w, :].T.astype(BF16)

    @pl.when(qb == last)
    def _():
        part = dk_hbm.shape[0] // PARTS
        copies = []
        for i in range(2 * PARTS):
            src, dst, out = ((dk, keys, dk_hbm), (dv, values, dv_hbm))[i % 2]
            start = i // 2 * part

            def move(j, carry):
                r = pl.multiple_of(start + j * 16, 16)
                dst[pl.ds(r, 16), :] = src[pl.ds(r, 16), :].astype(BF16)
                return carry

            lax.fori_loop(0, part // 16, move, 0)
            copy = pltpu.make_async_copy(dst.at[pl.ds(start, part), :], out.at[pl.ds(start, part), :], in_sems.at[i])
            copy.start()
            copies.append(copy)
        for copy in copies:
            copy.wait()


def attention_bwd(tiles, q, dc, ctx, k, v, kmeta, qmeta, probs):
    rows, width = q.shape
    span = kmeta.shape[0]
    nq, nc = rows // QB, TILES
    vm = pltpu.VMEM
    hbm = pl.BlockSpec(memory_space=pl.ANY)
    full = lambda *s: pl.BlockSpec(s, lambda i, r: (0,) * len(s))
    block = pl.BlockSpec((QB, width), lambda i, r: (i, 0))
    shape = jax.ShapeDtypeStruct
    return pl.pallas_call(
        bwd_kernel,
        grid_spec=pltpu.PrefetchScalarGridSpec(
            num_scalar_prefetch=1, grid=(nq,),
            in_specs=[block] * 3 + [hbm] * 2 + [full(span, 128), pl.BlockSpec((8, QB), lambda i, r: (0, i)), hbm],
            out_specs=[block, hbm, hbm, full(16, 160)],
            scratch_shapes=[
                vm((span, width), BF16), vm((span, width), BF16),
                vm((span, width), F32), vm((span, width), F32), vm((width, QB), F32),
                vm((3, KB, QB), F32), vm((16 * KB, QB), F32), vm((8, 2 * QB), F32),
                vm((PAIRS, 2 * QB, 128), BF16), vm((PAIRS, 2 * QB, 128), BF16),
                vm((2, PAIRS, KB, 2 * QB), BF16), pltpu.SemaphoreType.DMA((2,)), pltpu.SemaphoreType.DMA((2 * PARTS,))]),
        out_shape=[shape((rows, width), BF16), shape(k.shape, BF16), shape(k.shape, BF16), shape((16, 160), F32)],
        compiler_params=pltpu.CompilerParams(vmem_limit_bytes=56 * 2**20, dimension_semantics=("arbitrary",)),
        cost_estimate=pl.CostEstimate(flops=40 * 10**9, bytes_accessed=40 * 2**20, transcendentals=0),
        name="attention_backward",
    )(tiles, q, dc, ctx, k, v, kmeta, qmeta, probs)


REACH = 560


def exchange_plan(n_seq, n_ffn, half):
    seq_bits = [("seq", 1 << b) for b in range(n_seq.bit_length() - 1)]
    ffn_bits = [("ffn", 1 << b) for b in range(1, n_ffn.bit_length() - 1)]
    unit = 16 * n_seq * n_ffn // 2
    if (n_seq, n_ffn) == (2, 16) and half % (6 * unit) == 0:
        x, y, z, far = seq_bits + ffn_bits
        orders = [[x, y, z, far], [y, z, far, x], [far, x, y, z], [z, x, y, far], [x, z, far, y], [y, x, z, far]]
        return orders, half // 6
    return [seq_bits + ffn_bits], half


def sum_kernel(orders, length, n_ffn, dq_ref, context_ref, attn_ref, small_ref, table_ref,
               window_hbm, dk_hbm, dv_hbm, wq_hbm, wk_hbm, wv_hbm, mid_hbm, out_ref, small_out, hidden_ref,
               window_ref, dk_ref, dv_ref, wq_ref, wk_ref, wv_ref, mid_ref, load_sems, a_ref, halo_out, halo_in, work, core_in, slots, sums, small_in,
               halo_send, halo_recv, core_sems, core_back, send_sems, recv_sems, back_send, back_recv, small_send, small_recv):
    seq, ffn = lax.axis_index("seq"), lax.axis_index("ffn")
    loads = [
        pltpu.make_async_copy(src, dst, load_sems.at[i])
        for i, (src, dst) in enumerate((
            (window_hbm, window_ref), (dk_hbm, dk_ref), (dv_hbm, dv_ref), (wk_hbm, wk_ref), (wv_hbm, wv_ref), (wq_hbm, wq_ref), (mid_hbm, mid_ref),
        ))
    ]
    for load in loads:
        load.start()
    half = work.shape[0]
    streams = len(orders)
    steps = len(orders[0])
    core = lax.rem(ffn, 2)

    def bit_of(axis, bit):
        return lax.rem((seq if axis == "seq" else ffn) // bit, 2)

    def partner(axis, bit):
        flip = bit * (1 - 2 * bit_of(axis, bit))
        return {axis: (seq if axis == "seq" else ffn) + flip}

    peers = [("ffn", 1)] + sorted(orders[0])
    barrier = pltpu.get_barrier_semaphore()
    for axis, bit in peers:
        pl.semaphore_signal(barrier, inc=1, device_id=partner(axis, bit), device_id_type=pl.DeviceIdType.MESH)
    has_low, has_high = ffn > 0, ffn < n_ffn - 1
    pl.semaphore_signal(barrier, inc=1, device_id={"ffn": lax.rem(ffn + 2 * core - 1 + n_ffn, n_ffn)},
                        device_id_type=pl.DeviceIdType.MESH)

    rows = dq_ref.shape[0]
    span, width = window_ref.shape
    pairs = width // 256

    def gradient(place, left, first, right, scale):
        depth = right.shape[0]

        def block(j, carry):
            part = tn(left[first : first + depth, pl.ds(pl.multiple_of(j * 128, 128), 128)], right[...])
            row = lax.rem(j, 2) * half + (place * pairs + j // 2) * 128
            a_ref[pl.ds(pl.multiple_of(row, 128), 128), :] = (part * scale).astype(BF16)
            return carry

        lax.fori_loop(0, width // 128, block, 0)

    gradient(0, context_ref, 0, attn_ref, 1.0)
    for load in loads:
        load.wait()
    gradient(1, window_ref, rows, dq_ref, 0.125)
    sums[0] = small_ref[...]
    sums[0, 8:24, 0 : table_ref.shape[1]] = table_ref[...]
    ones = jnp.ones((16, span), BF16)
    sums[0, 0:1, :] = nn(ones[:, :rows], dq_ref[...])[0:1] * 0.125
    sums[0, 1:2, :] = nn(ones, dv_ref[...])[0:1]

    pl.semaphore_wait(barrier, len(peers) + 1)

    def remote(src, dst, send, recv, axis, bit):
        return pltpu.make_async_remote_copy(src_ref=src, dst_ref=dst, send_sem=send, recv_sem=recv,
                                            device_id=partner(axis, bit), device_id_type=pl.DeviceIdType.MESH)

    def at(ref, start, size):
        return ref.at[pl.ds(start if isinstance(start, int) else pl.multiple_of(start, 16), size), :]

    def add(dst, dst_lo, one, one_lo, two, two_lo, size):
        def body(i, carry):
            r = i * 16
            dst[pl.ds(pl.multiple_of(dst_lo + r, 16), 16), :] = (
                one[pl.ds(pl.multiple_of(one_lo + r, 16), 16), :].astype(F32)
                + two[pl.ds(pl.multiple_of(two_lo + r, 16), 16), :].astype(F32)
            ).astype(BF16)
            return carry
        lax.fori_loop(0, size // 16, body, 0)

    pending = []
    firsts = []
    ready = 2 * pairs * 128
    late = [lambda: gradient(2, window_ref, 0, dk_ref, 1.0), lambda: gradient(3, window_ref, 0, dv_ref, 1.0)]
    for s in range(streams):
        while ready < (s + 1) * length and late:
            late.pop(0)()
            ready += pairs * 128
        copy = remote(at(a_ref, (1 - core) * half + s * length, length), at(core_in, s * length, length),
                      core_sems.at[s], core_sems.at[streams + s], "ffn", 1)
        copy.start()
        firsts.append(copy)

    def small_copy(k):
        axis, bit = peers[k]
        return remote(sums.at[k], small_in.at[k], small_send.at[k], small_recv.at[k], axis, bit)
    small_copy(0).start()

    def halo_copy(side):
        return pltpu.make_async_remote_copy(
            src_ref=halo_out.at[side], dst_ref=halo_in.at[side], send_sem=halo_send.at[side], recv_sem=halo_recv.at[side],
            device_id={"ffn": ffn + (2 * side - 1)}, device_id_type=pl.DeviceIdType.MESH)

    for side, first in ((0, rows - REACH), (1, 2 * rows)):
        def through(j, carry):
            r = pl.multiple_of(j * 112, 16)
            near = pl.ds(pl.multiple_of(first + r, 16), 112)
            part = nt(dk_ref[near, :], wk_ref[...]) + nt(dv_ref[near, :], wv_ref[...])
            halo_out[side, pl.ds(r, 112), :] = part.astype(BF16)
            return carry

        lax.fori_loop(0, REACH // 112, through, 0)

        @pl.when((has_low, has_high)[side])
        def _():
            halo_copy(side).start()

    lows = [s * length for s in range(streams)]
    sizes = [length] * streams
    offs = []
    base = 0
    for s in range(streams):
        own = []
        size = length
        for k in range(steps):
            size //= 2
            own.append((base, size))
            base += size
        offs.append(own)

    def scatter(s, k):
        axis, bit = orders[s][k]
        size = sizes[s] // 2
        mine = lows[s] + bit_of(axis, bit) * size
        theirs = lows[s] + (1 - bit_of(axis, bit)) * size
        slot, _ = offs[s][k]
        copy = remote(at(work, theirs, size), at(slots, slot, size), send_sems.at[s, k], recv_sems.at[s, k], axis, bit)
        copy.start()
        return copy, mine, size

    flying = []
    for s in range(streams):
        firsts[s].wait_recv()
        add(work, s * length, a_ref, core * half + s * length, core_in, s * length, length)
        flying.append(scatter(s, 0))

    def own_rows(j, carry):
        r = pl.multiple_of(j * 128, 128)
        here, there = pl.ds(r, 128), pl.ds(pl.multiple_of(rows + r, 128), 128)
        hidden_ref[here, :] = (
            mid_ref[here, :] + nt(dq_ref[here, :], wq_ref[...]) * 0.125
            + nt(dk_ref[there, :], wk_ref[...]) + nt(dv_ref[there, :], wv_ref[...])
        )
        return carry

    lax.fori_loop(0, rows // 128, own_rows, 0)
    for k in range(steps):
        for s in range(streams):
            copy, mine, size = flying[s]
            copy.wait_recv()
            slot, _ = offs[s][k]
            last = k == steps - 1
            if last:
                add(out_ref, core * half + mine, work, mine, slots, slot, size)
            else:
                add(work, mine, work, mine, slots, slot, size)
            pending.append(copy)
            lows[s], sizes[s] = mine, size
            if not last:
                flying[s] = scatter(s, k + 1)
            else:
                flying[s] = gather(s, k, lows, sizes, orders, remote, at, out_ref, core, half, back_send, back_recv)
        small_copy(k).wait_recv()
        sums[k + 1] = sums[k] + small_in[k]
        small_copy(k + 1).start()
    small_copy(steps).wait_recv()
    small_out[...] = sums[steps] + small_in[steps]
    for side, there in ((1, has_low), (0, has_high)):
        @pl.when(there)
        def _():
            pltpu.make_async_remote_copy(
                src_ref=halo_out.at[side], dst_ref=halo_in.at[side], send_sem=halo_send.at[side], recv_sem=halo_recv.at[side],
                device_id={"ffn": ffn - (2 * side - 1)}, device_id_type=pl.DeviceIdType.MESH).wait_recv()

            def merge(j, carry):
                there = pl.ds(pl.multiple_of(j * 16, 16), 16)
                r = pl.ds(pl.multiple_of((1 - side) * (rows - REACH) + j * 16, 16), 16)
                hidden_ref[r, :] = hidden_ref[r, :] + halo_in[side, there, :].astype(F32)
                return carry

            lax.fori_loop(0, REACH // 16, merge, 0)
    finals = []
    for k in range(steps - 1, -1, -1):
        for s in range(streams):
            copy = flying[s]
            copy.wait_recv()
            pending.append(copy)
            axis, bit = orders[s][k]
            lows[s] = lows[s] - bit_of(axis, bit) * sizes[s]
            sizes[s] = 2 * sizes[s]
            if k:
                flying[s] = gather(s, k - 1, lows, sizes, orders, remote, at, out_ref, core, half, back_send, back_recv)
            else:
                copy = remote(at(out_ref, core * half + s * length, length), at(out_ref, core * half + s * length, length),
                              core_back.at[s], core_back.at[streams + s], "ffn", 1)
                copy.start()
                finals.append(copy)
    for copy in finals:
        copy.wait_recv()
    for copy in firsts + pending + finals:
        copy.wait_send()
    for k in range(steps + 1):
        small_copy(k).wait_send()
    for side, there in ((0, has_low), (1, has_high)):
        @pl.when(there)
        def _():
            halo_copy(side).wait_send()


def gather(s, k, lows, sizes, orders, remote, at, out_ref, core, half, back_send, back_recv):
    axis, bit = orders[s][k]
    place = at(out_ref, core * half + lows[s], sizes[s])
    copy = remote(place, place, back_send.at[s, k], back_recv.at[s, k], axis, bit)
    copy.start()
    return copy


def sum_everywhere(window, dq, dk, dv, context, attn, wq, wk, wv, mid, small, table):
    n_seq, n_ffn = lax.axis_size("seq"), lax.axis_size("ffn")
    grain = 16 * n_seq * n_ffn // 2
    rows, width = dq.shape
    half = -(-(2 * width) // grain) * grain
    orders, length = exchange_plan(n_seq, n_ffn, half)
    streams, steps = len(orders), len(orders[0])
    vm, dma = pltpu.VMEM, pltpu.SemaphoreType.DMA
    slot_rows = streams * (length - length // (1 << steps))
    shape = jax.ShapeDtypeStruct
    held = lambda a: vm(a.shape, a.dtype)
    return pl.pallas_call(
        functools.partial(sum_kernel, orders, length, n_ffn),
        out_shape=[shape((2 * half, width), BF16), shape(small.shape, F32), shape((rows, width), F32)],
        in_specs=[pl.BlockSpec(memory_space=vm)] * 5 + [pl.BlockSpec(memory_space=pl.ANY)] * 7,
        out_specs=[pl.BlockSpec(memory_space=vm)] * 3,
        scratch_shapes=[
            held(window), held(dk), held(dv), held(wq), held(wk), held(wv), held(mid), dma((7,)),
            vm((2 * half, width), BF16), vm((2, REACH, width), BF16), vm((2, REACH, width), BF16),
            vm((half, width), BF16), vm((half, width), BF16), vm((slot_rows, width), BF16),
            vm((steps + 1,) + small.shape, F32), vm((steps + 1,) + small.shape, F32),
            dma((2,)), dma((2,)),
            dma((2 * streams,)), dma((2 * streams,)), dma((streams, steps)), dma((streams, steps)),
            dma((streams, steps)), dma((streams, steps)), dma((steps + 1,)), dma((steps + 1,)),
        ],
        compiler_params=pltpu.CompilerParams(collective_id=0, has_side_effects=True, vmem_limit_bytes=58 * 2**20),
        cost_estimate=pl.CostEstimate(flops=15 * 10**9, bytes_accessed=30 * 2**20, transcendentals=0),
        name="sum_everywhere",
    )(dq, context, attn, small, table, window, dk, dv, wq, wk, wv, mid)


UB = 512


def gelu_and_slope(x):
    z = jnp.abs(x) * 0.7071067811865476
    t = 1.0 / (1.0 + 0.3275911 * z)
    poly = ((((1.061405429 * t - 1.453152027) * t + 1.421413741) * t - 0.284496736) * t + 0.254829592) * t
    bell = jnp.exp(-z * z)
    tail = 0.5 * poly * bell
    phi = jnp.where(x < 0, tail, 1.0 - tail)
    return x * phi, phi + x * bell * 0.3989422804014327


def tn(a, b):
    return lax.dot_general(a, b, (((0,), (0,)), ((), ())), preferred_element_type=F32)


def ffn_up_kernel(normed_ref, up_ref, active_ref, slope_ref):
    rows = normed_ref.shape[0]
    size = rows // 2
    for r in range(0, rows, size):
        w = slice(r, r + size)
        act, slope = gelu_and_slope(nt(normed_ref[w, :], up_ref[...]))
        active_ref[w, :] = act.astype(BF16)
        slope_ref[w, :] = slope.astype(BF16)


def ffn_up(normed, up):
    rows, wide = normed.shape
    units = up.shape[0]
    full = lambda *s: pl.BlockSpec(s, lambda i: (0,) * len(s))
    col = pl.BlockSpec((rows, UB), lambda i: (0, i))
    shape = jax.ShapeDtypeStruct
    return pl.pallas_call(
        ffn_up_kernel,
        grid=(units // UB,),
        in_specs=[full(rows, wide), pl.BlockSpec((UB, wide), lambda i: (i, 0))],
        out_specs=[col, col],
        out_shape=[shape((rows, units), BF16), shape((rows, units), BF16)],
        compiler_params=pltpu.CompilerParams(vmem_limit_bytes=48 * 2**20, dimension_semantics=("arbitrary",)),
        cost_estimate=pl.CostEstimate(flops=2 * rows * units * wide, bytes_accessed=15 * 2**20, transcendentals=2 * rows * units),
        name="ffn_up",
    )(normed, up)


def ffn_back_kernel(grad_ref, normed_ref, up_ref, down_ref, active_ref, slope_ref, unit_ref, bias_ref, normed_grad_ref):
    @pl.when(pl.program_id(0) == 0)
    def _():
        normed_grad_ref[...] = jnp.zeros_like(normed_grad_ref)

    grad = grad_ref[...]
    width = grad.shape[1]
    unit_ref[:, width:] = tn(active_ref[...], grad).astype(BF16)
    pre = (nt(grad, down_ref[...]) * slope_ref[...].astype(F32)).astype(BF16)
    up_grad = tn(pre, normed_ref[...])
    unit_ref[:, :width] = up_grad[:, :width].astype(BF16)
    bias_ref[...] = up_grad[:, width:]
    normed_grad_ref[...] = normed_grad_ref[...] + nn(pre, up_ref[:, :width])


def ffn_back(grad, normed, up, down, active, slope):
    rows, wide = normed.shape
    units, width = down.shape
    full = lambda *s: pl.BlockSpec(s, lambda i: (0,) * len(s))
    col = pl.BlockSpec((rows, UB), lambda i: (0, i))
    row = lambda n: pl.BlockSpec((UB, n), lambda i: (i, 0))
    shape = jax.ShapeDtypeStruct
    return pl.pallas_call(
        ffn_back_kernel,
        grid=(units // UB,),
        in_specs=[full(rows, width), full(rows, wide), row(wide), row(width), col, col],
        out_specs=[row(2 * width), row(wide - width), full(rows, width)],
        out_shape=[shape((units, 2 * width), BF16), shape((units, wide - width), F32), shape((rows, width), F32)],
        compiler_params=pltpu.CompilerParams(vmem_limit_bytes=48 * 2**20, dimension_semantics=("arbitrary",)),
        cost_estimate=pl.CostEstimate(flops=4 * rows * units * (wide + width), bytes_accessed=30 * 2**20, transcendentals=0),
        name="ffn_back",
    )(grad, normed, up, down, active, slope)


def layer_norm(value, gain, shift):
    center = value - jnp.mean(value, axis=-1, keepdims=True)
    spread = jnp.mean(center * center, axis=-1, keepdims=True)
    return center * lax.rsqrt(spread + norm_eps) * gain + shift


def layout(row_ids, doc_ends):
    forwarded_value = row_ids[:, None] >= doc_ends[None, :]
    doc_ids = jnp.sum(forwarded_value.astype(jnp.int32), axis=1)
    starts = jnp.max(jnp.where(forwarded_value, doc_ends[None, :], 0), axis=1)
    offsets = row_ids - starts
    places = jnp.where(offsets < VISUAL, offsets, offsets - VISUAL)
    return (doc_ids, places)


def tile_table(starts, doc_ids, key_docs, window_start, rows):
    docs = jnp.arange(starts.shape[0] - 1, dtype=jnp.int32)
    place = jnp.arange(doc_ids.shape[0], dtype=jnp.int32)
    ends = jnp.max(jnp.where(key_docs[None, :] == docs[:, None], place[None, :] + 1, 0), axis=1)
    own = doc_ids[rows : 2 * rows]
    segments = own[0::QB, None] + jnp.arange(3, dtype=jnp.int32)[None, :]
    active = segments <= own[QB - 1 :: QB, None]
    hit = segments[:, :, None] == docs[None, None, :]
    low = jnp.sum(jnp.where(hit, starts[None, None, :-1], 0), axis=2) - window_start
    low = jnp.maximum(low, 0) // 16 * 16
    high = jnp.sum(jnp.where(hit, ends[None, None, :], 0), axis=2)
    count = jnp.where(active, jnp.maximum(high - low + KB - 1, 0) // KB, 0)
    before = jnp.cumsum(count, axis=1) - count
    index = jnp.arange(TILES, dtype=jnp.int32)[None, None, :] - before[:, :, None]
    inside = (index >= 0) & (index < count[:, :, None])
    base = jnp.sum(jnp.where(inside, low[:, :, None] + KB * index, 0), axis=1)
    doc = jnp.sum(jnp.where(inside, segments[:, :, None], 0), axis=1)
    return jnp.concatenate([jnp.sum(count, axis=1, keepdims=True), base, doc], axis=1).astype(jnp.int32)


def on_device(
    hidden_in, doc_lengths, box_x, box_y, token_valid, w_query, b_query, w_key, w_value, b_value,
    w_out, b_out, gain_attn, shift_attn, w_up, b_up, w_down, b_down, gain_out, shift_out,
    table_seq, table_x, table_y, out_grad,
):
    rows = hidden_in.shape[0]
    width = hidden_in.shape[1]
    heads = table_seq.shape[1]
    group_rows = box_x.shape[0]
    span = 3 * rows
    first_row = lax.axis_index("ffn") * rows
    doc_ends = jnp.cumsum(doc_lengths[0])

    n_ffn = lax.axis_size("ffn")
    n_seq = lax.axis_size("seq")
    up = [(i, i + 1) for i in range(n_ffn - 1)]
    hidden_low = lax.ppermute(hidden_in, "ffn", up)
    hidden_high = lax.ppermute(hidden_in, "ffn", [(j, i) for i, j in up])

    units = b_up.shape[0]
    up_ext = jnp.concatenate([w_up.T, b_up[:, None], jnp.zeros((units, 127), BF16)], axis=1)
    later, up_ext = lax.optimization_barrier((w_down, up_ext))
    up_all = lax.all_gather(up_ext, "ffn", axis=0, tiled=True)
    down_all = lax.all_gather(later, "ffn", axis=0, tiled=True)

    window_rows = first_row - rows + jnp.arange(span, dtype=jnp.int32)
    doc_ids, places = layout(window_rows, doc_ends)
    inside = (window_rows >= 0) & (window_rows < group_rows)

    def window_of(item):
        edge = jnp.zeros((rows,), item.dtype)
        padded = jnp.concatenate([edge, item, edge])
        return lax.dynamic_slice_in_dim(padded, first_row, span)

    win_x, win_y = window_of(box_x), window_of(box_y)
    key_open = (window_of(token_valid) == 1) & inside
    key_docs = jnp.where(key_open, doc_ids, -1)
    kmeta = jnp.stack([places, win_x, win_y, key_docs], axis=1).astype(F32)
    kmeta = jnp.pad(kmeta, ((0, KB), (0, 124)), constant_values=-1.0)
    own = slice(rows, 2 * rows)
    qmeta = jnp.stack([places[own], win_x[own], win_y[own], doc_ids[own]], axis=0).astype(F32)
    qmeta = jnp.pad(qmeta, ((0, 4), (0, 0)))
    starts = jnp.concatenate([jnp.zeros((1,), doc_ends.dtype), doc_ends])
    tiles = tile_table(starts, doc_ids, key_docs, first_row - rows, rows)
    tables = order_tables(table_seq, table_x, table_y)

    query = ((jnp.dot(hidden_in, w_query, preferred_element_type=F32) + b_query) * 0.125).astype(BF16)
    window = jnp.concatenate([hidden_low, hidden_in, hidden_high], axis=0)
    key = jnp.dot(window, w_key, preferred_element_type=F32).astype(BF16)
    value = (jnp.dot(window, w_value, preferred_element_type=F32) + b_value).astype(BF16)

    context, inv, probs = attention_fwd(tiles, query, key, value, kmeta, qmeta, tables)
    context_low = context.astype(BF16)
    attn = jnp.dot(context_low, w_out, preferred_element_type=F32) + b_out
    inputs = hidden_in.astype(F32)
    normed, norm_pull = jax.vjp(
        layer_norm, inputs + attn, gain_attn.astype(F32), shift_attn.astype(F32)
    )
    normed_low = normed.astype(BF16)
    ones = jnp.concatenate([jnp.ones((rows, 1), BF16), jnp.zeros((rows, 127), BF16)], axis=1)
    normed_ext = jnp.concatenate([normed_low, ones], axis=1)
    active, slope = ffn_up(normed_ext, up_all)
    branch = jnp.dot(active, down_all, preferred_element_type=F32)
    hidden_out, out_pull = jax.vjp(
        layer_norm, normed + (branch + b_down), gain_out.astype(F32), shift_out.astype(F32)
    )
    mid_grad, grad_gain_out, grad_shift_out = out_pull(out_grad.astype(F32))
    branch_grad = mid_grad.astype(BF16)
    grad_b_down = jnp.sum(branch_grad.astype(F32), axis=0)
    unit_part, bias_part, branch_back = ffn_back(branch_grad, normed_ext, up_all, down_all, active, slope)
    unit_grad = lax.psum_scatter(unit_part, "ffn", scatter_dimension=0, tiled=True)
    normed_grad = mid_grad + branch_back
    mid1_grad, grad_gain_attn, grad_shift_attn = norm_pull(normed_grad)
    attn_grad = mid1_grad.astype(BF16)
    grad_b_out = jnp.sum(attn_grad.astype(F32), axis=0)
    scaled = (nt(attn_grad, w_out) * inv).astype(BF16)
    query_grad, key_grad, value_grad, table_sum = attention_bwd(
        tiles, query, scaled, context, key, value, kmeta, qmeta, probs
    )
    small = jnp.stack(
        [
            jnp.zeros_like(grad_b_out),
            jnp.zeros_like(grad_b_out),
            grad_b_out,
            grad_gain_attn,
            grad_shift_attn,
            grad_b_down,
            grad_gain_out,
            grad_shift_out,
        ]
    )
    levels = table_sum.shape[1]
    small = jnp.concatenate(
        [small, jnp.zeros((16, width), F32), bias_part[:, 0].reshape(-1, width)], axis=0
    )
    big, small, hidden_grad = sum_everywhere(
        window, query_grad, key_grad, value_grad, context_low, attn_grad, w_query, w_key, w_value, mid1_grad, small, table_sum
    )
    big, small, unit_grad = lax.optimization_barrier((big, small, unit_grad))
    for b in range(n_seq.bit_length() - 1):
        unit_grad = unit_grad + lax.ppermute(unit_grad, "seq", [(i, i ^ (1 << b)) for i in range(n_seq)])
    unit_grad = unit_grad.astype(F32)
    grad_w_up = unit_grad[:, :width].T
    grad_w_down = unit_grad[:, width:]
    grad_b_up = lax.dynamic_slice_in_dim(small[24:].reshape(-1), lax.axis_index("ffn") * units, units)
    blocks = big.reshape(2, -1, width)[:, : 2 * width].reshape(2, 4, -1, 128, width)
    g_out, g_query, g_key, g_value = [
        jnp.stack([blocks[0, m], blocks[1, m]], axis=1).reshape(width, width).astype(F32) for m in range(4)
    ]
    grads = [g_query, g_key, g_value, g_out]
    vec = [small[i] for i in range(8)]
    table_all = jnp.stack([small[8 + h // 2 + 8 * (h % 2), :levels] for h in range(heads)], axis=1)
    return (
        hidden_out, hidden_grad, grads[0], vec[0], grads[1], grads[2], vec[1], grads[3], vec[2], vec[3], vec[4],
        grad_w_up, grad_b_up, grad_w_down, vec[5], vec[6], vec[7],
        table_all[:32], table_all[32:96], table_all[96:],
    )


def solution(mesh):
    in_specs = (
        P(("seq", "ffn"), None),
        P("seq", None),
        P("seq"),
        P("seq"),
        P("seq"),
        P(),
        P(),
        P(),
        P(),
        P(),
        P(),
        P(),
        P(),
        P(),
        P(None, "ffn"),
        P("ffn"),
        P("ffn", None),
        P(),
        P(),
        P(),
        P(),
        P(),
        P(),
        P(("seq", "ffn"), None),
    )
    out_specs = (
        P(("seq", "ffn"), None),
        P(("seq", "ffn"), None),
        P(),
        P(),
        P(),
        P(),
        P(),
        P(),
        P(),
        P(),
        P(),
        P(None, "ffn"),
        P("ffn"),
        P("ffn", None),
        P(),
        P(),
        P(),
        P(),
        P(),
        P(),
    )
    return jax.shard_map(
        on_device, mesh=mesh, in_specs=in_specs, out_specs=out_specs, check_vma=False
    )
```

```python
import functools

import jax
import jax.numpy as jnp
from jax import lax
from jax.experimental import pallas as pl
from jax.experimental.pallas import tpu as pltpu
from jax.sharding import PartitionSpec as P

VISUAL = 49
norm_eps = 1e-12
F32 = jnp.float32
BF16 = jnp.bfloat16
QB = 128
KB = 128
RB = 16
PAIRS = 6
NEG = -1e30
TILES = 12


def nn(a, b):
    return lax.dot_general(a, b, (((1,), (0,)), ((), ())), preferred_element_type=F32)


def nt(a, b):
    return lax.dot_general(a, b, (((1,), (1,)), ((), ())), preferred_element_type=F32)


def log_bucket(d, near, per_octave, sign):
    mag = jnp.abs(d)
    far = jnp.floor(jnp.log2(jnp.maximum(mag, 1.0) * (1.0 / near)) * per_octave + 0.0002) + near
    far = jnp.minimum(far, 2.0 * near - 1.0)
    return jnp.where(mag < near, mag, far) + jnp.where(d > 0, F32(sign), F32(0))


def put_buckets(b_ref, kmeta, qmeta, doc):
    key_doc = jnp.where(kmeta[:, 3:4] == doc.astype(F32), kmeta[:, 3:4], -1.0)
    same = key_doc == qmeta[3:4, :]
    b_ref[0] = jnp.where(same, log_bucket(kmeta[:, 0:1] - qmeta[0:1, :], 8.0, 2.0, 16.0), 16.0)
    b_ref[1] = log_bucket(kmeta[:, 1:2] - qmeta[1:2, :], 16.0, 4.0, 32.0)
    b_ref[2] = log_bucket(kmeta[:, 2:3] - qmeta[2:3, :], 16.0, 4.0, 32.0)


def one_hot(b_ref, row, count):
    cols = []
    for r in range(count):
        parts = []
        for t, size in ((0, 32), (1, 64), (2, 64)):
            v = jnp.broadcast_to(b_ref[t, pl.ds(row + r, 1), :], (size, QB)).astype(BF16)
            levels = lax.broadcasted_iota(jnp.int32, (size, QB), 0).astype(F32).astype(BF16)
            parts.append(jnp.where(v == levels, BF16(1), BF16(0)))
        cols.append(jnp.concatenate(parts, axis=0))
    return jnp.concatenate(cols, axis=1)


def fill_stack(stack, src):
    lane = lax.broadcasted_iota(jnp.int32, (QB, 128), 1)
    for p in range(PAIRS):
        x = src[:, 128 * p : 128 * p + 128].astype(F32)
        stack[p, 0:QB, :] = jnp.where(lane < 64, x, 0.0).astype(BF16)
        stack[p, QB : 2 * QB, :] = jnp.where(lane < 64, 0.0, x).astype(BF16)


PARTS = 8


def window_copies(k_hbm, v_hbm, keys, values, sems):
    part = k_hbm.shape[0] // PARTS
    return [
        pltpu.make_async_copy(
            (k_hbm, v_hbm)[j].at[pl.ds(i * part, part), :], (keys, values)[j].at[pl.ds(i * part, part), :], sems.at[2 * i + j]
        )
        for i in range(PARTS)
        for j in range(2)
    ]


def clear_tail(keys, values):
    for ref in (keys, values):
        ref[ref.shape[0] - KB :, :] = jnp.zeros((KB, ref.shape[1]), ref.dtype)


def tile_of(tiles, qb, t):
    return pl.multiple_of(tiles[qb, 1 + t], 16), tiles[qb, 1 + TILES + t]


def fwd_kernel(tiles, q_ref, k_hbm, v_hbm, kmeta_ref, qmeta_ref, tab_ref, ctx_ref, inv_ref, p_hbm,
               keys, values, s_scr, b_scr, bias_scr, qstack, ctx_t, m_scr, l_scr, pbuf, sems, in_sems):
    qb = pl.program_id(0)
    count = tiles[qb, 0]

    @pl.when(qb == 0)
    def _():
        copies = window_copies(k_hbm, v_hbm, keys, values, in_sems)
        for copy in copies:
            copy.start()
        clear_tail(keys, values)
        for copy in copies:
            copy.wait()

    fill_stack(qstack, q_ref)
    m_scr[...] = jnp.full_like(m_scr, -3e38)
    l_scr[...] = jnp.zeros_like(l_scr)
    ctx_t[...] = jnp.zeros_like(ctx_t)
    tab = tab_ref[...]

    def pass1(c, carry):
        base, doc = tile_of(tiles, qb, c)
        put_buckets(b_scr, kmeta_ref[pl.ds(base, KB), :], qmeta_ref[...], doc)

        def rows(g, carry):
            j = g * RB
            out = nn(tab, one_hot(b_scr, j, RB))
            for r in range(RB):
                bias_scr[pl.ds(j + r, 16, stride=KB), :] = out[:, r * QB : (r + 1) * QB]
            return carry

        lax.fori_loop(0, KB // RB, rows, 0, unroll=KB // RB)
        for p in range(PAIRS):
            raw = nt(keys[pl.ds(base, KB), 128 * p : 128 * p + 128], qstack[p])
            o = 8 + p
            s = raw + jnp.concatenate([bias_scr[p * KB : (p + 1) * KB, :], bias_scr[o * KB : (o + 1) * KB, :]], axis=1)
            s_scr[c, p] = s
            m_scr[p] = jnp.maximum(m_scr[p], jnp.max(s.reshape(KB // 8, 8, 2 * QB), axis=0))
        return carry

    lax.fori_loop(0, count, pass1, 0)
    for p in range(PAIRS):
        m_scr[p] = jnp.broadcast_to(jnp.max(m_scr[p], axis=0, keepdims=True), (8, 2 * QB))

    def pcopy(slot, c):
        return pltpu.make_async_copy(pbuf.at[slot], p_hbm.at[qb, c], sems.at[slot])

    def pass2(c, carry):
        base, _ = tile_of(tiles, qb, c)
        slot = lax.rem(c, 2)

        @pl.when(c >= 2)
        def _():
            pcopy(slot, c).wait()

        for p in range(PAIRS):
            e = jnp.exp(s_scr[c, p] - m_scr[p, 0:1, :])
            l_scr[p] = l_scr[p] + jnp.sum(e.reshape(KB // 8, 8, 2 * QB), axis=0)
            pb = e.astype(BF16)
            pbuf[slot, p] = pb
            value_t = values[pl.ds(base, KB), 128 * p : 128 * p + 128].T
            for h in range(2):
                r = 128 * p + 64 * h
                ctx_t[r : r + 64, :] = ctx_t[r : r + 64, :] + nn(value_t[64 * h : 64 * h + 64], pb[:, h * QB : (h + 1) * QB])
        pcopy(slot, c).start()
        return carry

    lax.fori_loop(0, count, pass2, 0)
    for p in range(PAIRS):
        inv = 1.0 / jnp.sum(l_scr[p], axis=0, keepdims=True)
        wide = jnp.concatenate([jnp.broadcast_to(inv[:, :QB], (64, QB)), jnp.broadcast_to(inv[:, QB:], (64, QB))], axis=0)
        w = slice(128 * p, 128 * p + 128)
        ctx_ref[:, w] = (ctx_t[w, :] * wide).T
        inv_ref[:, w] = wide.T

    @pl.when(count >= 2)
    def _():
        pcopy(lax.rem(count, 2), 0).wait()

    pcopy(lax.rem(count + 1, 2), 0).wait()


def attention_fwd(tiles, q, k, v, kmeta, qmeta, tab):
    rows, width = q.shape
    span = kmeta.shape[0]
    nq, nc = rows // QB, TILES
    vm = pltpu.VMEM
    hbm = pl.BlockSpec(memory_space=pl.ANY)
    full = lambda *s: pl.BlockSpec(s, lambda i, r: (0,) * len(s))
    block = pl.BlockSpec((QB, width), lambda i, r: (i, 0))
    return pl.pallas_call(
        fwd_kernel,
        grid_spec=pltpu.PrefetchScalarGridSpec(
            num_scalar_prefetch=1, grid=(nq,),
            in_specs=[block] + [hbm] * 2 + [full(span, 128), pl.BlockSpec((8, QB), lambda i, r: (0, i)), full(16, 160)],
            out_specs=[block, block, hbm],
            scratch_shapes=[
                vm((span, width), BF16), vm((span, width), BF16),
                vm((nc, PAIRS, KB, 2 * QB), F32), vm((3, KB, QB), F32), vm((16 * KB, QB), F32),
                vm((PAIRS, 2 * QB, 128), BF16), vm((width, QB), F32), vm((PAIRS, 8, 2 * QB), F32),
                vm((PAIRS, 8, 2 * QB), F32), vm((2, PAIRS, KB, 2 * QB), BF16),
                pltpu.SemaphoreType.DMA((2,)), pltpu.SemaphoreType.DMA((2 * PARTS,))]),
        out_shape=[jax.ShapeDtypeStruct((rows, width), F32), jax.ShapeDtypeStruct((rows, width), F32),
                   jax.ShapeDtypeStruct((nq, nc, PAIRS, KB, 2 * QB), BF16)],
        compiler_params=pltpu.CompilerParams(vmem_limit_bytes=56 * 2**20, dimension_semantics=("arbitrary",)),
        cost_estimate=pl.CostEstimate(flops=25 * 10**9, bytes_accessed=30 * 2**20, transcendentals=5 * 10**6),
        name="attention_forward",
    )(tiles, q, k, v, kmeta, qmeta, tab)


def order_tables(ts, tx, ty):
    t = jnp.concatenate([ts.at[16].set(NEG), tx, ty], axis=0).T
    z = jnp.zeros((2, 160), t.dtype)
    return jnp.concatenate([t[0::2], z, t[1::2], z], axis=0)


def bwd_kernel(tiles, q_ref, dc_ref, ctx_ref, k_hbm, v_hbm, kmeta_ref, qmeta_ref, p_hbm,
               dq_ref, dk_hbm, dv_hbm, dtab_ref,
               keys, values, dk, dv, dq_t, b_scr, ds_scr, delta, qstack, cstack, pbuf, sems, in_sems):
    qb = pl.program_id(0)
    last = pl.num_programs(0) - 1
    count = tiles[qb, 0]

    before = jnp.int32(0)
    for b in range(dk.shape[0] // (3 * QB)):
        before = before + jnp.where(b < qb, tiles[b, 0], 0)

    def pcopy(block, c, slot):
        return pltpu.make_async_copy(p_hbm.at[block, c], pbuf.at[slot], sems.at[slot])

    @pl.when(qb == 0)
    def _():
        pcopy(0, 0, 0).start()
        copies = window_copies(k_hbm, v_hbm, keys, values, in_sems)
        for copy in copies:
            copy.start()
        clear_tail(keys, values)
        dk[...] = jnp.zeros_like(dk)
        dv[...] = jnp.zeros_like(dv)
        dtab_ref[...] = jnp.zeros_like(dtab_ref)
        ds_scr[...] = jnp.zeros_like(ds_scr)
        for copy in copies:
            copy.wait()

    fill_stack(qstack, q_ref)
    fill_stack(cstack, dc_ref)
    for p in range(PAIRS):
        w = slice(128 * p, 128 * p + 128)
        both = (dc_ref[:, w].astype(F32) * ctx_ref[:, w]).T
        delta[p : p + 1, :] = jnp.concatenate(
            [jnp.sum(both[:64], axis=0, keepdims=True), jnp.sum(both[64:], axis=0, keepdims=True)], axis=1)
    dq_t[...] = jnp.zeros_like(dq_t)

    def tile(c, carry):
        base, doc = tile_of(tiles, qb, c)
        slot = lax.rem(before + c, 2)

        @pl.when(c + 1 < count)
        def _():
            pcopy(qb, c + 1, 1 - slot).start()

        @pl.when((c + 1 == count) & (qb < last))
        def _():
            pcopy(qb + 1, 0, 1 - slot).start()

        put_buckets(b_scr, kmeta_ref[pl.ds(base, KB), :], qmeta_ref[...], doc)
        pcopy(qb, c, slot).wait()
        for p in range(PAIRS):
            w = slice(128 * p, 128 * p + 128)
            dp = nt(values[pl.ds(base, KB), w], cstack[p])
            pb = pbuf[slot, p]
            ds = pb.astype(F32) * (dp - delta[p : p + 1, :])
            ds_scr[p * KB : (p + 1) * KB, :] = ds[:, :QB]
            ds_scr[(8 + p) * KB : (9 + p) * KB, :] = ds[:, QB:]
            dsb = ds.astype(BF16)
            dk[pl.ds(base, KB), w] = dk[pl.ds(base, KB), w] + nn(dsb, qstack[p])
            dv[pl.ds(base, KB), w] = dv[pl.ds(base, KB), w] + nn(pb, cstack[p])
            key_t = keys[pl.ds(base, KB), w].T
            for h in range(2):
                r = 128 * p + 64 * h
                dq_t[r : r + 64, :] = dq_t[r : r + 64, :] + nn(key_t[64 * h : 64 * h + 64], dsb[:, h * QB : (h + 1) * QB])

        def rows(g, acc):
            j = g * RB
            d = jnp.concatenate([ds_scr[pl.ds(j + r, 16, stride=KB), :] for r in range(RB)], axis=1).astype(BF16)
            return acc + nt(d, one_hot(b_scr, j, RB))

        dtab_ref[...] = lax.fori_loop(0, KB // RB, rows, dtab_ref[...], unroll=KB // RB)
        return carry

    lax.fori_loop(0, count, tile, 0)
    for p in range(PAIRS):
        w = slice(128 * p, 128 * p + 128)
        dq_ref[:, w] = dq_t[w, :].T.astype(BF16)

    @pl.when(qb == last)
    def _():
        part = dk_hbm.shape[0] // PARTS
        copies = []
        for i in range(2 * PARTS):
            src, dst, out = ((dk, keys, dk_hbm), (dv, values, dv_hbm))[i % 2]
            start = i // 2 * part

            def move(j, carry):
                r = pl.multiple_of(start + j * 16, 16)
                dst[pl.ds(r, 16), :] = src[pl.ds(r, 16), :].astype(BF16)
                return carry

            lax.fori_loop(0, part // 16, move, 0)
            copy = pltpu.make_async_copy(dst.at[pl.ds(start, part), :], out.at[pl.ds(start, part), :], in_sems.at[i])
            copy.start()
            copies.append(copy)
        for copy in copies:
            copy.wait()


def attention_bwd(tiles, q, dc, ctx, k, v, kmeta, qmeta, probs):
    rows, width = q.shape
    span = kmeta.shape[0]
    nq, nc = rows // QB, TILES
    vm = pltpu.VMEM
    hbm = pl.BlockSpec(memory_space=pl.ANY)
    full = lambda *s: pl.BlockSpec(s, lambda i, r: (0,) * len(s))
    block = pl.BlockSpec((QB, width), lambda i, r: (i, 0))
    shape = jax.ShapeDtypeStruct
    return pl.pallas_call(
        bwd_kernel,
        grid_spec=pltpu.PrefetchScalarGridSpec(
            num_scalar_prefetch=1, grid=(nq,),
            in_specs=[block] * 3 + [hbm] * 2 + [full(span, 128), pl.BlockSpec((8, QB), lambda i, r: (0, i)), hbm],
            out_specs=[block, hbm, hbm, full(16, 160)],
            scratch_shapes=[
                vm((span, width), BF16), vm((span, width), BF16),
                vm((span, width), F32), vm((span, width), F32), vm((width, QB), F32),
                vm((3, KB, QB), F32), vm((16 * KB, QB), F32), vm((8, 2 * QB), F32),
                vm((PAIRS, 2 * QB, 128), BF16), vm((PAIRS, 2 * QB, 128), BF16),
                vm((2, PAIRS, KB, 2 * QB), BF16), pltpu.SemaphoreType.DMA((2,)), pltpu.SemaphoreType.DMA((2 * PARTS,))]),
        out_shape=[shape((rows, width), BF16), shape(k.shape, BF16), shape(k.shape, BF16), shape((16, 160), F32)],
        compiler_params=pltpu.CompilerParams(vmem_limit_bytes=56 * 2**20, dimension_semantics=("arbitrary",)),
        cost_estimate=pl.CostEstimate(flops=40 * 10**9, bytes_accessed=40 * 2**20, transcendentals=0),
        name="attention_backward",
    )(tiles, q, dc, ctx, k, v, kmeta, qmeta, probs)


REACH = 560


def exchange_plan(n_seq, n_ffn, half):
    seq_bits = [("seq", 1 << b) for b in range(n_seq.bit_length() - 1)]
    ffn_bits = [("ffn", 1 << b) for b in range(1, n_ffn.bit_length() - 1)]
    unit = 16 * n_seq * n_ffn // 2
    if (n_seq, n_ffn) == (2, 16) and half % (6 * unit) == 0:
        x, y, z, far = seq_bits + ffn_bits
        orders = [[x, y, z, far], [y, z, far, x], [far, x, y, z], [z, x, y, far], [x, z, far, y], [y, x, z, far]]
        return orders, half // 6
    return [seq_bits + ffn_bits], half


def sum_kernel(orders, length, n_ffn, dq_ref, context_ref, attn_ref, small_ref, table_ref,
               window_hbm, dk_hbm, dv_hbm, wq_hbm, wk_hbm, wv_hbm, mid_hbm, out_ref, small_out, hidden_ref,
               window_ref, dk_ref, dv_ref, wq_ref, wk_ref, wv_ref, mid_ref, load_sems, a_ref, halo_out, halo_in, work, core_in, slots, sums, small_in,
               halo_send, halo_recv, core_sems, core_back, send_sems, recv_sems, back_send, back_recv, small_send, small_recv):
    seq, ffn = lax.axis_index("seq"), lax.axis_index("ffn")
    loads = [
        pltpu.make_async_copy(src, dst, load_sems.at[i])
        for i, (src, dst) in enumerate((
            (window_hbm, window_ref), (dk_hbm, dk_ref), (dv_hbm, dv_ref), (wk_hbm, wk_ref), (wv_hbm, wv_ref), (wq_hbm, wq_ref), (mid_hbm, mid_ref),
        ))
    ]
    for load in loads:
        load.start()
    half = work.shape[0]
    streams = len(orders)
    steps = len(orders[0])
    core = lax.rem(ffn, 2)

    def bit_of(axis, bit):
        return lax.rem((seq if axis == "seq" else ffn) // bit, 2)

    def partner(axis, bit):
        flip = bit * (1 - 2 * bit_of(axis, bit))
        return {axis: (seq if axis == "seq" else ffn) + flip}

    peers = [("ffn", 1)] + sorted(orders[0])
    barrier = pltpu.get_barrier_semaphore()
    for axis, bit in peers:
        pl.semaphore_signal(barrier, inc=1, device_id=partner(axis, bit), device_id_type=pl.DeviceIdType.MESH)
    has_low, has_high = ffn > 0, ffn < n_ffn - 1
    pl.semaphore_signal(barrier, inc=1, device_id={"ffn": lax.rem(ffn + 2 * core - 1 + n_ffn, n_ffn)},
                        device_id_type=pl.DeviceIdType.MESH)

    rows = dq_ref.shape[0]
    span, width = window_ref.shape
    pairs = width // 256

    def gradient(place, left, first, right, scale):
        depth = right.shape[0]

        def block(j, carry):
            part = tn(left[first : first + depth, pl.ds(pl.multiple_of(j * 128, 128), 128)], right[...])
            row = lax.rem(j, 2) * half + (place * pairs + j // 2) * 128
            a_ref[pl.ds(pl.multiple_of(row, 128), 128), :] = (part * scale).astype(BF16)
            return carry

        lax.fori_loop(0, width // 128, block, 0)

    gradient(0, context_ref, 0, attn_ref, 1.0)
    for load in loads:
        load.wait()
    gradient(1, window_ref, rows, dq_ref, 0.125)
    sums[0] = small_ref[...]
    sums[0, 8:24, 0 : table_ref.shape[1]] = table_ref[...]
    ones = jnp.ones((16, span), BF16)
    sums[0, 0:1, :] = nn(ones[:, :rows], dq_ref[...])[0:1] * 0.125
    sums[0, 1:2, :] = nn(ones, dv_ref[...])[0:1]

    pl.semaphore_wait(barrier, len(peers) + 1)

    def remote(src, dst, send, recv, axis, bit):
        return pltpu.make_async_remote_copy(src_ref=src, dst_ref=dst, send_sem=send, recv_sem=recv,
                                            device_id=partner(axis, bit), device_id_type=pl.DeviceIdType.MESH)

    def at(ref, start, size):
        return ref.at[pl.ds(start if isinstance(start, int) else pl.multiple_of(start, 16), size), :]

    def add(dst, dst_lo, one, one_lo, two, two_lo, size):
        def body(i, carry):
            r = i * 16
            dst[pl.ds(pl.multiple_of(dst_lo + r, 16), 16), :] = (
                one[pl.ds(pl.multiple_of(one_lo + r, 16), 16), :].astype(F32)
                + two[pl.ds(pl.multiple_of(two_lo + r, 16), 16), :].astype(F32)
            ).astype(BF16)
            return carry
        lax.fori_loop(0, size // 16, body, 0)

    pending = []
    firsts = []
    ready = 2 * pairs * 128
    late = [lambda: gradient(2, window_ref, 0, dk_ref, 1.0), lambda: gradient(3, window_ref, 0, dv_ref, 1.0)]
    for s in range(streams):
        while ready < (s + 1) * length and late:
            late.pop(0)()
            ready += pairs * 128
        copy = remote(at(a_ref, (1 - core) * half + s * length, length), at(core_in, s * length, length),
                      core_sems.at[s], core_sems.at[streams + s], "ffn", 1)
        copy.start()
        firsts.append(copy)

    def small_copy(k):
        axis, bit = peers[k]
        return remote(sums.at[k], small_in.at[k], small_send.at[k], small_recv.at[k], axis, bit)
    small_copy(0).start()

    def halo_copy(side):
        return pltpu.make_async_remote_copy(
            src_ref=halo_out.at[side], dst_ref=halo_in.at[side], send_sem=halo_send.at[side], recv_sem=halo_recv.at[side],
            device_id={"ffn": ffn + (2 * side - 1)}, device_id_type=pl.DeviceIdType.MESH)

    for side, first in ((0, rows - REACH), (1, 2 * rows)):
        def through(j, carry):
            r = pl.multiple_of(j * 112, 16)
            near = pl.ds(pl.multiple_of(first + r, 16), 112)
            part = nt(dk_ref[near, :], wk_ref[...]) + nt(dv_ref[near, :], wv_ref[...])
            halo_out[side, pl.ds(r, 112), :] = part.astype(BF16)
            return carry

        lax.fori_loop(0, REACH // 112, through, 0)

        @pl.when((has_low, has_high)[side])
        def _():
            halo_copy(side).start()

    lows = [s * length for s in range(streams)]
    sizes = [length] * streams
    offs = []
    base = 0
    for s in range(streams):
        own = []
        size = length
        for k in range(steps):
            size //= 2
            own.append((base, size))
            base += size
        offs.append(own)

    def scatter(s, k):
        axis, bit = orders[s][k]
        size = sizes[s] // 2
        mine = lows[s] + bit_of(axis, bit) * size
        theirs = lows[s] + (1 - bit_of(axis, bit)) * size
        slot, _ = offs[s][k]
        copy = remote(at(work, theirs, size), at(slots, slot, size), send_sems.at[s, k], recv_sems.at[s, k], axis, bit)
        copy.start()
        return copy, mine, size

    flying = []
    for s in range(streams):
        firsts[s].wait_recv()
        add(work, s * length, a_ref, core * half + s * length, core_in, s * length, length)
        flying.append(scatter(s, 0))

    def own_rows(j, carry):
        r = pl.multiple_of(j * 128, 128)
        here, there = pl.ds(r, 128), pl.ds(pl.multiple_of(rows + r, 128), 128)
        hidden_ref[here, :] = (
            mid_ref[here, :] + nt(dq_ref[here, :], wq_ref[...]) * 0.125
            + nt(dk_ref[there, :], wk_ref[...]) + nt(dv_ref[there, :], wv_ref[...])
        )
        return carry

    lax.fori_loop(0, rows // 128, own_rows, 0)
    for k in range(steps):
        for s in range(streams):
            copy, mine, size = flying[s]
            copy.wait_recv()
            slot, _ = offs[s][k]
            last = k == steps - 1
            if last:
                add(out_ref, core * half + mine, work, mine, slots, slot, size)
            else:
                add(work, mine, work, mine, slots, slot, size)
            pending.append(copy)
            lows[s], sizes[s] = mine, size
            if not last:
                flying[s] = scatter(s, k + 1)
            else:
                flying[s] = gather(s, k, lows, sizes, orders, remote, at, out_ref, core, half, back_send, back_recv)
        small_copy(k).wait_recv()
        sums[k + 1] = sums[k] + small_in[k]
        small_copy(k + 1).start()
    small_copy(steps).wait_recv()
    small_out[...] = sums[steps] + small_in[steps]
    for side, there in ((1, has_low), (0, has_high)):
        @pl.when(there)
        def _():
            pltpu.make_async_remote_copy(
                src_ref=halo_out.at[side], dst_ref=halo_in.at[side], send_sem=halo_send.at[side], recv_sem=halo_recv.at[side],
                device_id={"ffn": ffn - (2 * side - 1)}, device_id_type=pl.DeviceIdType.MESH).wait_recv()

            def merge(j, carry):
                there = pl.ds(pl.multiple_of(j * 16, 16), 16)
                r = pl.ds(pl.multiple_of((1 - side) * (rows - REACH) + j * 16, 16), 16)
                hidden_ref[r, :] = hidden_ref[r, :] + halo_in[side, there, :].astype(F32)
                return carry

            lax.fori_loop(0, REACH // 16, merge, 0)
    finals = []
    for k in range(steps - 1, -1, -1):
        for s in range(streams):
            copy = flying[s]
            copy.wait_recv()
            pending.append(copy)
            axis, bit = orders[s][k]
            lows[s] = lows[s] - bit_of(axis, bit) * sizes[s]
            sizes[s] = 2 * sizes[s]
            if k:
                flying[s] = gather(s, k - 1, lows, sizes, orders, remote, at, out_ref, core, half, back_send, back_recv)
            else:
                copy = remote(at(out_ref, core * half + s * length, length), at(out_ref, core * half + s * length, length),
                              core_back.at[s], core_back.at[streams + s], "ffn", 1)
                copy.start()
                finals.append(copy)
    for copy in finals:
        copy.wait_recv()
    for copy in firsts + pending + finals:
        copy.wait_send()
    for k in range(steps + 1):
        small_copy(k).wait_send()
    for side, there in ((0, has_low), (1, has_high)):
        @pl.when(there)
        def _():
            halo_copy(side).wait_send()


def gather(s, k, lows, sizes, orders, remote, at, out_ref, core, half, back_send, back_recv):
    axis, bit = orders[s][k]
    place = at(out_ref, core * half + lows[s], sizes[s])
    copy = remote(place, place, back_send.at[s, k], back_recv.at[s, k], axis, bit)
    copy.start()
    return copy


def sum_everywhere(window, dq, dk, dv, context, attn, wq, wk, wv, mid, small, table):
    n_seq, n_ffn = lax.axis_size("seq"), lax.axis_size("ffn")
    grain = 16 * n_seq * n_ffn // 2
    rows, width = dq.shape
    half = -(-(2 * width) // grain) * grain
    orders, length = exchange_plan(n_seq, n_ffn, half)
    streams, steps = len(orders), len(orders[0])
    vm, dma = pltpu.VMEM, pltpu.SemaphoreType.DMA
    slot_rows = streams * (length - length // (1 << steps))
    shape = jax.ShapeDtypeStruct
    held = lambda a: vm(a.shape, a.dtype)
    return pl.pallas_call(
        functools.partial(sum_kernel, orders, length, n_ffn),
        out_shape=[shape((2 * half, width), BF16), shape(small.shape, F32), shape((rows, width), F32)],
        in_specs=[pl.BlockSpec(memory_space=vm)] * 5 + [pl.BlockSpec(memory_space=pl.ANY)] * 7,
        out_specs=[pl.BlockSpec(memory_space=vm)] * 3,
        scratch_shapes=[
            held(window), held(dk), held(dv), held(wq), held(wk), held(wv), held(mid), dma((7,)),
            vm((2 * half, width), BF16), vm((2, REACH, width), BF16), vm((2, REACH, width), BF16),
            vm((half, width), BF16), vm((half, width), BF16), vm((slot_rows, width), BF16),
            vm((steps + 1,) + small.shape, F32), vm((steps + 1,) + small.shape, F32),
            dma((2,)), dma((2,)),
            dma((2 * streams,)), dma((2 * streams,)), dma((streams, steps)), dma((streams, steps)),
            dma((streams, steps)), dma((streams, steps)), dma((steps + 1,)), dma((steps + 1,)),
        ],
        compiler_params=pltpu.CompilerParams(collective_id=0, has_side_effects=True, vmem_limit_bytes=58 * 2**20),
        cost_estimate=pl.CostEstimate(flops=15 * 10**9, bytes_accessed=30 * 2**20, transcendentals=0),
        name="sum_everywhere",
    )(dq, context, attn, small, table, window, dk, dv, wq, wk, wv, mid)


UB = 768


def gelu_and_slope(x):
    z = jnp.abs(x) * 0.7071067811865476
    t = 1.0 / (1.0 + 0.3275911 * z)
    poly = ((((1.061405429 * t - 1.453152027) * t + 1.421413741) * t - 0.284496736) * t + 0.254829592) * t
    bell = jnp.exp(-z * z)
    tail = 0.5 * poly * bell
    phi = jnp.where(x < 0, tail, 1.0 - tail)
    return x * phi, phi + x * bell * 0.3989422804014327


def tn(a, b):
    return lax.dot_general(a, b, (((0,), (0,)), ((), ())), preferred_element_type=F32)


def ffn_up_kernel(normed_ref, up_ref, active_ref, slope_ref):
    rows = normed_ref.shape[0]
    size = rows // 2
    for r in range(0, rows, size):
        w = slice(r, r + size)
        act, slope = gelu_and_slope(nt(normed_ref[w, :], up_ref[...]))
        active_ref[w, :] = act.astype(BF16)
        slope_ref[w, :] = slope.astype(BF16)


def ffn_up(normed, up):
    rows, wide = normed.shape
    units = up.shape[0]
    full = lambda *s: pl.BlockSpec(s, lambda i: (0,) * len(s))
    col = pl.BlockSpec((rows, UB), lambda i: (0, i))
    shape = jax.ShapeDtypeStruct
    return pl.pallas_call(
        ffn_up_kernel,
        grid=(units // UB,),
        in_specs=[full(rows, wide), pl.BlockSpec((UB, wide), lambda i: (i, 0))],
        out_specs=[col, col],
        out_shape=[shape((rows, units), BF16), shape((rows, units), BF16)],
        compiler_params=pltpu.CompilerParams(vmem_limit_bytes=48 * 2**20, dimension_semantics=("arbitrary",)),
        cost_estimate=pl.CostEstimate(flops=2 * rows * units * wide, bytes_accessed=15 * 2**20, transcendentals=2 * rows * units),
        name="ffn_up",
    )(normed, up)


def ffn_back_kernel(grad_ref, normed_ref, up_ref, down_ref, active_ref, slope_ref, unit_ref, bias_ref, normed_grad_ref):
    @pl.when(pl.program_id(0) == 0)
    def _():
        normed_grad_ref[...] = jnp.zeros_like(normed_grad_ref)

    grad = grad_ref[...]
    width = grad.shape[1]
    unit_ref[:, width:] = tn(active_ref[...], grad).astype(BF16)
    pre = (nt(grad, down_ref[...]) * slope_ref[...].astype(F32)).astype(BF16)
    up_grad = tn(pre, normed_ref[...])
    unit_ref[:, :width] = up_grad[:, :width].astype(BF16)
    bias_ref[...] = up_grad[:, width:]
    normed_grad_ref[...] = normed_grad_ref[...] + nn(pre, up_ref[:, :width])


def ffn_back(grad, normed, up, down, active, slope):
    rows, wide = normed.shape
    units, width = down.shape
    full = lambda *s: pl.BlockSpec(s, lambda i: (0,) * len(s))
    col = pl.BlockSpec((rows, UB), lambda i: (0, i))
    row = lambda n: pl.BlockSpec((UB, n), lambda i: (i, 0))
    shape = jax.ShapeDtypeStruct
    return pl.pallas_call(
        ffn_back_kernel,
        grid=(units // UB,),
        in_specs=[full(rows, width), full(rows, wide), row(wide), row(width), col, col],
        out_specs=[row(2 * width), row(wide - width), full(rows, width)],
        out_shape=[shape((units, 2 * width), BF16), shape((units, wide - width), F32), shape((rows, width), F32)],
        compiler_params=pltpu.CompilerParams(vmem_limit_bytes=48 * 2**20, dimension_semantics=("arbitrary",)),
        cost_estimate=pl.CostEstimate(flops=4 * rows * units * (wide + width), bytes_accessed=30 * 2**20, transcendentals=0),
        name="ffn_back",
    )(grad, normed, up, down, active, slope)


def layer_norm(value, gain, shift):
    center = value - jnp.mean(value, axis=-1, keepdims=True)
    spread = jnp.mean(center * center, axis=-1, keepdims=True)
    return center * lax.rsqrt(spread + norm_eps) * gain + shift


def layout(row_ids, doc_ends):
    forwarded_value = row_ids[:, None] >= doc_ends[None, :]
    doc_ids = jnp.sum(forwarded_value.astype(jnp.int32), axis=1)
    starts = jnp.max(jnp.where(forwarded_value, doc_ends[None, :], 0), axis=1)
    offsets = row_ids - starts
    places = jnp.where(offsets < VISUAL, offsets, offsets - VISUAL)
    return (doc_ids, places)


def tile_table(starts, doc_ids, key_docs, window_start, rows):
    docs = jnp.arange(starts.shape[0] - 1, dtype=jnp.int32)
    place = jnp.arange(doc_ids.shape[0], dtype=jnp.int32)
    ends = jnp.max(jnp.where(key_docs[None, :] == docs[:, None], place[None, :] + 1, 0), axis=1)
    own = doc_ids[rows : 2 * rows]
    segments = own[0::QB, None] + jnp.arange(3, dtype=jnp.int32)[None, :]
    active = segments <= own[QB - 1 :: QB, None]
    hit = segments[:, :, None] == docs[None, None, :]
    low = jnp.sum(jnp.where(hit, starts[None, None, :-1], 0), axis=2) - window_start
    low = jnp.maximum(low, 0) // 16 * 16
    high = jnp.sum(jnp.where(hit, ends[None, None, :], 0), axis=2)
    count = jnp.where(active, jnp.maximum(high - low + KB - 1, 0) // KB, 0)
    before = jnp.cumsum(count, axis=1) - count
    index = jnp.arange(TILES, dtype=jnp.int32)[None, None, :] - before[:, :, None]
    inside = (index >= 0) & (index < count[:, :, None])
    base = jnp.sum(jnp.where(inside, low[:, :, None] + KB * index, 0), axis=1)
    doc = jnp.sum(jnp.where(inside, segments[:, :, None], 0), axis=1)
    return jnp.concatenate([jnp.sum(count, axis=1, keepdims=True), base, doc], axis=1).astype(jnp.int32)


def on_device(
    hidden_in, doc_lengths, box_x, box_y, token_valid, w_query, b_query, w_key, w_value, b_value,
    w_out, b_out, gain_attn, shift_attn, w_up, b_up, w_down, b_down, gain_out, shift_out,
    table_seq, table_x, table_y, out_grad,
):
    rows = hidden_in.shape[0]
    width = hidden_in.shape[1]
    heads = table_seq.shape[1]
    group_rows = box_x.shape[0]
    span = 3 * rows
    first_row = lax.axis_index("ffn") * rows
    doc_ends = jnp.cumsum(doc_lengths[0])

    n_ffn = lax.axis_size("ffn")
    n_seq = lax.axis_size("seq")
    up = [(i, i + 1) for i in range(n_ffn - 1)]
    hidden_low = lax.ppermute(hidden_in, "ffn", up)
    hidden_high = lax.ppermute(hidden_in, "ffn", [(j, i) for i, j in up])

    units = b_up.shape[0]
    up_ext = jnp.concatenate([w_up.T, b_up[:, None], jnp.zeros((units, 127), BF16)], axis=1)
    later, up_ext = lax.optimization_barrier((w_down, up_ext))
    up_all = lax.all_gather(up_ext, "ffn", axis=0, tiled=True)
    down_all = lax.all_gather(later, "ffn", axis=0, tiled=True)

    window_rows = first_row - rows + jnp.arange(span, dtype=jnp.int32)
    doc_ids, places = layout(window_rows, doc_ends)
    inside = (window_rows >= 0) & (window_rows < group_rows)

    def window_of(item):
        edge = jnp.zeros((rows,), item.dtype)
        padded = jnp.concatenate([edge, item, edge])
        return lax.dynamic_slice_in_dim(padded, first_row, span)

    win_x, win_y = window_of(box_x), window_of(box_y)
    key_open = (window_of(token_valid) == 1) & inside
    key_docs = jnp.where(key_open, doc_ids, -1)
    kmeta = jnp.stack([places, win_x, win_y, key_docs], axis=1).astype(F32)
    kmeta = jnp.pad(kmeta, ((0, KB), (0, 124)), constant_values=-1.0)
    own = slice(rows, 2 * rows)
    qmeta = jnp.stack([places[own], win_x[own], win_y[own], doc_ids[own]], axis=0).astype(F32)
    qmeta = jnp.pad(qmeta, ((0, 4), (0, 0)))
    starts = jnp.concatenate([jnp.zeros((1,), doc_ends.dtype), doc_ends])
    tiles = tile_table(starts, doc_ids, key_docs, first_row - rows, rows)
    tables = order_tables(table_seq, table_x, table_y)

    query = ((jnp.dot(hidden_in, w_query, preferred_element_type=F32) + b_query) * 0.125).astype(BF16)
    window = jnp.concatenate([hidden_low, hidden_in, hidden_high], axis=0)
    key = jnp.dot(window, w_key, preferred_element_type=F32).astype(BF16)
    value = (jnp.dot(window, w_value, preferred_element_type=F32) + b_value).astype(BF16)

    context, inv, probs = attention_fwd(tiles, query, key, value, kmeta, qmeta, tables)
    context_low = context.astype(BF16)
    attn = jnp.dot(context_low, w_out, preferred_element_type=F32) + b_out
    inputs = hidden_in.astype(F32)
    normed, norm_pull = jax.vjp(
        layer_norm, inputs + attn, gain_attn.astype(F32), shift_attn.astype(F32)
    )
    normed_low = normed.astype(BF16)
    ones = jnp.concatenate([jnp.ones((rows, 1), BF16), jnp.zeros((rows, 127), BF16)], axis=1)
    normed_ext = jnp.concatenate([normed_low, ones], axis=1)
    active, slope = ffn_up(normed_ext, up_all)
    branch = jnp.dot(active, down_all, preferred_element_type=F32)
    hidden_out, out_pull = jax.vjp(
        layer_norm, normed + (branch + b_down), gain_out.astype(F32), shift_out.astype(F32)
    )
    mid_grad, grad_gain_out, grad_shift_out = out_pull(out_grad.astype(F32))
    branch_grad = mid_grad.astype(BF16)
    grad_b_down = jnp.sum(branch_grad.astype(F32), axis=0)
    unit_part, bias_part, branch_back = ffn_back(branch_grad, normed_ext, up_all, down_all, active, slope)
    unit_grad = lax.psum_scatter(unit_part, "ffn", scatter_dimension=0, tiled=True)
    normed_grad = mid_grad + branch_back
    mid1_grad, grad_gain_attn, grad_shift_attn = norm_pull(normed_grad)
    attn_grad = mid1_grad.astype(BF16)
    grad_b_out = jnp.sum(attn_grad.astype(F32), axis=0)
    scaled = (nt(attn_grad, w_out) * inv).astype(BF16)
    query_grad, key_grad, value_grad, table_sum = attention_bwd(
        tiles, query, scaled, context, key, value, kmeta, qmeta, probs
    )
    small = jnp.stack(
        [
            jnp.zeros_like(grad_b_out),
            jnp.zeros_like(grad_b_out),
            grad_b_out,
            grad_gain_attn,
            grad_shift_attn,
            grad_b_down,
            grad_gain_out,
            grad_shift_out,
        ]
    )
    levels = table_sum.shape[1]
    small = jnp.concatenate(
        [small, jnp.zeros((16, width), F32), bias_part[:, 0].reshape(-1, width)], axis=0
    )
    big, small, hidden_grad = sum_everywhere(
        window, query_grad, key_grad, value_grad, context_low, attn_grad, w_query, w_key, w_value, mid1_grad, small, table_sum
    )
    big, small, unit_grad = lax.optimization_barrier((big, small, unit_grad))
    for b in range(n_seq.bit_length() - 1):
        unit_grad = unit_grad + lax.ppermute(unit_grad, "seq", [(i, i ^ (1 << b)) for i in range(n_seq)])
    unit_grad = unit_grad.astype(F32)
    grad_w_up = unit_grad[:, :width].T
    grad_w_down = unit_grad[:, width:]
    grad_b_up = lax.dynamic_slice_in_dim(small[24:].reshape(-1), lax.axis_index("ffn") * units, units)
    blocks = big.reshape(2, -1, width)[:, : 2 * width].reshape(2, 4, -1, 128, width)
    g_out, g_query, g_key, g_value = [
        jnp.stack([blocks[0, m], blocks[1, m]], axis=1).reshape(width, width).astype(F32) for m in range(4)
    ]
    grads = [g_query, g_key, g_value, g_out]
    vec = [small[i] for i in range(8)]
    table_all = jnp.stack([small[8 + h // 2 + 8 * (h % 2), :levels] for h in range(heads)], axis=1)
    return (
        hidden_out, hidden_grad, grads[0], vec[0], grads[1], grads[2], vec[1], grads[3], vec[2], vec[3], vec[4],
        grad_w_up, grad_b_up, grad_w_down, vec[5], vec[6], vec[7],
        table_all[:32], table_all[32:96], table_all[96:],
    )


def solution(mesh):
    in_specs = (
        P(("seq", "ffn"), None),
        P("seq", None),
        P("seq"),
        P("seq"),
        P("seq"),
        P(),
        P(),
        P(),
        P(),
        P(),
        P(),
        P(),
        P(),
        P(),
        P(None, "ffn"),
        P("ffn"),
        P("ffn", None),
        P(),
        P(),
        P(),
        P(),
        P(),
        P(),
        P(("seq", "ffn"), None),
    )
    out_specs = (
        P(("seq", "ffn"), None),
        P(("seq", "ffn"), None),
        P(),
        P(),
        P(),
        P(),
        P(),
        P(),
        P(),
        P(),
        P(),
        P(None, "ffn"),
        P("ffn"),
        P("ffn", None),
        P(),
        P(),
        P(),
        P(),
        P(),
        P(),
    )
    return jax.shard_map(
        on_device, mesh=mesh, in_specs=in_specs, out_specs=out_specs, check_vma=False
    )
```
